32 devices in a mesh: section: 2 (over x), seq: 2 (over core), dp: 8 (over z, y).
Axes of the slice: x: 2, y: 2, z: 4, core: 2. Of those that a mesh axis runs over, the one named last changes fastest.
Arguments:
- tokens: bfloat16 [2, 8, 1024, 768], P(None, 'dp', 'seq'), may hold values from -6 to 6
- cotangent: bfloat16 [2, 8, 1024, 768], P(None, 'dp', 'seq'), may hold values from -6 to 6
- segments: int32 [2, 8, 1024], P(None, 'dp', 'seq'), may hold values from 0 to 2, as said below
- norm_gain: bfloat16 [2, 768], P('section', ('seq', 'dp')), may hold values from 0.099609375 to 1.8984375
- in_weight: bfloat16 [2, 768, 3352], P('section', ('seq', 'dp')), may hold values from -0.21875 to 0.21875
- conv_weight: bfloat16 [2, 4, 1792], P('section', None, ('seq', 'dp')), may hold values from -3 to 3
- conv_bias: bfloat16 [2, 1792], P('section', ('seq', 'dp')), may hold values from -3 to 3
- dt_bias: float32 [2, 24], P('section'), may hold values from -6.9 to -2.3
- decay_log: float32 [2, 24], P('section'), may hold values from 0 to 2.77
- skip_gain: float32 [2, 24], P('section'), may hold values from 0.5 to 1.5
- out_gain: bfloat16 [2, 1536], P('section', ('seq', 'dp')), may hold values from 0.099609375 to 1.8984375
- out_weight: bfloat16 [2, 1536, 768], P('section', ('seq', 'dp')), may hold values from -0.15625 to 0.15625
Outputs:
- section_outputs: bfloat16 [2, 2, 8, 1024, 768], P('section', None, 'dp', 'seq')
- input_grads: float32 [2, 2, 8, 1024, 768], P('section', None, 'dp', 'seq')
- grad_norm_gain: float32 [2, 768], P('section', ('seq', 'dp'))
- grad_in_weight: float32 [2, 768, 3352], P('section', ('seq', 'dp'))
- grad_conv_weight: float32 [2, 4, 1792], P('section', None, ('seq', 'dp'))
- grad_conv_bias: float32 [2, 1792], P('section', ('seq', 'dp'))
- grad_dt_bias: float32 [2, 24], P('section')
- grad_decay_log: float32 [2, 24], P('section')
- grad_skip_gain: float32 [2, 24], P('section')
- grad_out_gain: float32 [2, 1536], P('section', ('seq', 'dp'))
- grad_out_weight: float32 [2, 1536, 768], P('section', ('seq', 'dp'))
The draws below stay inside these ranges and needn't reach their ends.
Inputs may be any that keep to these rules, and one draw needn't show every extreme that they name: `segments`: each sequence's document numbers start at 0 and never fall along it; tokens with equal numbers form one document.
All inputs are finite; a program needn't handle non-finite values.
Results may differ from the reference program's by a relative error of at most 0.012.
Values may be sent and summed in bfloat16 or wider, within the bound.
No kernel may reach another device: no remote copies, remote signals or barrier semaphores. Data moves between devices by JAX's collectives and lax.ppermute only.
A program may use at most 384 MiB of HBM per device.

```python
from functools import partial
import jax
import jax.numpy as jnp
from jax import lax

D = 768
DI = 1536
N = 128
P_SIZE = 64
H = 24
CONV = 4
MB = 2
LENGTH = 1024
NCUT = 2
SEQ_DEV = 1
SECTIONS = 2
SEQS = 8
PIECE = 512
XC = 1792
PW = 3352


def draw_segments(key, part):
    key = jax.random.fold_in(key, 7)
    key_cuts, key_pick = jax.random.split(key)
    cut_points = jax.random.randint(key_cuts, (MB, SEQS, NCUT), 1, LENGTH)
    positions = jnp.arange(LENGTH)
    seg_ids = jnp.sum((cut_points[:, :, None, :] <= positions[None, None, :, None]).astype(jnp.int32), axis=-1)
    group_count = SEQS // SEQ_DEV
    chosen = jax.random.randint(key_pick, (group_count,), 0, MB * SEQ_DEV)
    micro_index = jnp.arange(MB)[:, None]
    seq_index = jnp.arange(SEQS)[None, :]
    local_index = micro_index * SEQ_DEV + seq_index % SEQ_DEV
    whole_doc = local_index == chosen[seq_index // SEQ_DEV]
    return jnp.where(whole_doc[..., None], 0, seg_ids).astype(jnp.int32)


def block_levels(stream_key, shape, cuts, smallest, largest):
    gain, own = 1.0, jax.random.fold_in(stream_key, 6)
    for dim, shards_of in cuts:
        heights = jnp.exp(jax.random.uniform(jax.random.fold_in(own, dim), (shards_of,), jnp.float32, smallest / len(cuts), largest / len(cuts)))
        gain = gain * jnp.repeat(heights, shape[dim] // shards_of).reshape([-1 if axis == dim else 1 for axis in range(len(shape))])
    return gain


def normal_values(stream_key, dims, scale, reach, cuts=(), dtype=jnp.bfloat16):
    factor_of = block_levels(stream_key, dims, cuts, -0.22, 0.18) if cuts else 1.0
    array = jax.random.normal(stream_key, dims, jnp.float32) * scale * factor_of
    return jnp.minimum(jnp.maximum(array, -reach), reach).astype(dtype)


def setup_inputs(seed: int = 0) -> dict:
    keys = jax.random.split(jax.random.key(seed), 13)
    return {
        "tokens": normal_values(keys[0], (MB, SEQS, LENGTH, D), 1.0, 6.0, ((1, 8), (2, 2))),
        "cotangent": normal_values(keys[1], (MB, SEQS, LENGTH, D), 1.0, 6.0, ((1, 8), (2, 2))),
        "segments": draw_segments(jax.random.fold_in(keys[12], 71), 0),
        "norm_gain": jnp.clip(1.0 + 0.18 * jax.random.normal(keys[3], (SECTIONS, D), jnp.float32), 0.099609375, 1.8984375).astype(jnp.bfloat16),
        "in_weight": normal_values(keys[4], (SECTIONS, D, PW), D ** -0.5, 0.21875, ((0, 2), (1, 16))),
        "conv_weight": normal_values(keys[5], (SECTIONS, CONV, XC), CONV ** -0.5, 3.0, ((0, 2), (2, 16))),
        "conv_bias": normal_values(keys[6], (SECTIONS, XC), 0.5, 3.0, ((0, 2), (1, 16))),
        "dt_bias": jnp.clip(-6.9 + 4.6000001430511475 * jax.random.uniform(keys[7], (SECTIONS, H), jnp.float32) ** block_levels(keys[7], (SECTIONS, H), ((0, 2),), -0.2, 0.2), -6.9, -2.3),
        "decay_log": jnp.clip(2.77 * jax.random.uniform(keys[8], (SECTIONS, H), jnp.float32) ** block_levels(keys[8], (SECTIONS, H), ((0, 2),), -0.2, 0.2), 0.0, 2.77),
        "skip_gain": jnp.clip(0.5 + 1.0 * jax.random.uniform(keys[9], (SECTIONS, H), jnp.float32) ** block_levels(keys[9], (SECTIONS, H), ((0, 2),), -0.2, 0.2), 0.5, 1.5),
        "out_gain": jnp.clip(1.0 + 0.18 * jax.random.normal(keys[10], (SECTIONS, DI), jnp.float32), 0.099609375, 1.8984375).astype(jnp.bfloat16),
        "out_weight": normal_values(keys[11], (SECTIONS, DI, D), DI ** -0.5, 0.15625, ((0, 2), (1, 16))),
    }


epsilon = 1e-05
highest = lax.Precision.HIGHEST

@jax.custom_vjp
def low(v):
    return lax.optimization_barrier(v.astype(jnp.bfloat16)).astype(jnp.float32)

@jax.custom_vjp
def low_back(v):
    return v

def low_keep(v):
    return (low(v), None)

def low_pass(kept, grad):
    return (grad,)

def back_keep(v):
    return (v, None)

def back_low(kept, grad):
    return (low(grad),)
low.defvjp(low_keep, low_pass)
low_back.defvjp(back_keep, back_low)

def rms_scale(values, gain_vector):
    return values * lax.rsqrt(lax.optimization_barrier(jnp.mean(values * values, -1, keepdims=True)) + epsilon) * gain_vector

def block_scan(skip_gain, carried, inputs):
    ssm_state, previous = carried
    x_in, b_in, c_in, step_size, log_decay, seg_ids = inputs
    pieces = step_size.shape[0]
    cum_decay = jnp.cumsum(log_decay, 0)
    positions = jnp.arange(pieces)
    same_doc = ((seg_ids[:, None] == seg_ids[None, :]) & (positions[:, None] >= positions[None, :])).astype(jnp.float32)
    decay_gap = cum_decay[:, None, :] - cum_decay[None, :, :]
    kernel = jnp.exp(jnp.where(same_doc[..., None] > 0, decay_gap, 0.0)) * same_doc[..., None]
    scores = jnp.dot(c_in, b_in.T, precision=highest)
    mixing = scores[..., None] * kernel * step_size[None, :, :]
    heads_x = x_in.reshape(pieces, H, P_SIZE)
    result = jnp.einsum('tsh,shp->thp', mixing, heads_x, precision=highest)
    carry_in = jnp.exp(cum_decay) * (seg_ids == previous).astype(jnp.float32)[:, None]
    result = result + carry_in[..., None] * jnp.einsum('hpn,tn->thp', ssm_state, c_in, precision=highest)
    result = result + skip_gain[:, None] * heads_x
    last_decay = cum_decay[-1]
    tail_weight = jnp.exp(last_decay[None, :] - cum_decay) * (seg_ids == seg_ids[-1]).astype(jnp.float32)[:, None] * step_size
    local_state = jnp.einsum('shp,sn->hpn', tail_weight[..., None] * heads_x, b_in, precision=highest)
    through = jnp.exp(last_decay) * (seg_ids[-1] == previous).astype(jnp.float32)
    return ((through[:, None, None] * ssm_state + local_state, seg_ids[-1]), result.reshape(pieces, DI))

def layer(source, seg_ids, weights):
    norm_gain, in_weight, conv_weight, conv_bias, dt_bias, decay_log, skip_gain, out_gain, out_weight = weights
    normed = low(rms_scale(source, norm_gain))
    projected = low_back(jnp.dot(normed, in_weight, precision=highest))
    channels = DI + 2 * N
    gate_z = projected[:, :DI]
    conv_in = projected[:, DI:DI + channels]
    dt_raw = projected[:, DI + channels:]
    padded = jnp.concatenate([jnp.zeros((CONV - 1, channels), jnp.float32), conv_in], 0)
    seg_pad = jnp.concatenate([jnp.zeros((CONV - 1,), jnp.int32) + seg_ids[0], seg_ids], 0)
    conv_out = conv_bias + jnp.zeros_like(conv_in)
    for offset in range(CONV):
        doc_match = (seg_pad[offset:offset + LENGTH] == seg_ids).astype(jnp.float32)
        conv_out = conv_out + conv_weight[offset] * padded[offset:offset + LENGTH] * doc_match[:, None]
    activated = jax.nn.silu(conv_out)
    x_in = activated[:, :DI]
    b_in = activated[:, DI:DI + N]
    c_in = activated[:, DI + N:]
    step_size = jax.nn.softplus(dt_raw + dt_bias)
    log_decay = -jnp.exp(decay_log) * step_size
    blocks = LENGTH // PIECE

    def into_blocks(values):
        return values.reshape((blocks, PIECE) + values.shape[1:])
    scan_step = jax.checkpoint(partial(block_scan, skip_gain))
    start = (jnp.zeros((H, P_SIZE, N), jnp.float32), seg_ids[0])
    ended, scanned = lax.scan(scan_step, start, (into_blocks(x_in), into_blocks(b_in), into_blocks(c_in), into_blocks(step_size), into_blocks(log_decay), into_blocks(seg_ids)))
    gated_out = scanned.reshape(LENGTH, DI) * jax.nn.silu(gate_z)
    normed_out = low(rms_scale(gated_out, out_gain))
    return source + jnp.dot(normed_out, out_weight, precision=highest)

def reference(tokens, cotangent, segments, norm_gain, in_weight, conv_weight, conv_bias, dt_bias, decay_log, skip_gain, out_gain, out_weight):
    params = tuple((value.astype(jnp.float32) for value in (norm_gain, in_weight, conv_weight, conv_bias, dt_bias, decay_log, skip_gain, out_gain, out_weight)))
    sources = tokens.reshape(MB * SEQS, LENGTH, D).astype(jnp.float32)
    grads_in = cotangent.reshape(MB * SEQS, LENGTH, D).astype(jnp.float32)
    seg_rows = segments.reshape(MB * SEQS, LENGTH).astype(jnp.int32)

    def one_sequence(grad_total, seq_item):
        source, grad_final, seg_ids = seq_item

        def both_layers(first_in, probe, weights):
            first_layer = tuple((value[0] for value in weights))
            second_layer = tuple((value[1] for value in weights))
            passed = low_back(low(layer(first_in, seg_ids, first_layer) + probe))
            return (passed, layer(passed, seg_ids, second_layer))
        outputs, pullback = jax.vjp(both_layers, source, jnp.zeros_like(source), params)
        grad_source, grad_probe, grad_params = pullback((jnp.zeros_like(source), grad_final))
        grad_total = jax.tree.map(jnp.add, grad_total, grad_params)
        return (grad_total, (outputs[0], outputs[1], grad_source, grad_probe))
    zero_grads = jax.tree.map(jnp.zeros_like, params)
    grad_total, stacked = lax.scan(one_sequence, zero_grads, (sources, grads_in, seg_rows))
    full_shape = (MB, SEQS, LENGTH, D)
    section_outputs = jnp.stack([stacked[0].reshape(full_shape), stacked[1].reshape(full_shape)]).astype(jnp.bfloat16)
    input_grads = jnp.stack([stacked[2].reshape(full_shape), stacked[3].reshape(full_shape)])
    return (section_outputs, input_grads, grad_total[0], grad_total[1], grad_total[2], grad_total[3], grad_total[4], grad_total[5], grad_total[6], grad_total[7], grad_total[8])
```

```python
from functools import partial

import jax
import jax.numpy as jnp
from jax import lax
from jax.experimental import pallas as pl
from jax.experimental.pallas import tpu as pltpu
from jax.sharding import PartitionSpec as P

DI = 1536
N = 128
XC = 1792
EPS = 1e-05
MASKED = -1e30
VMEM_LIMIT = 40 * 1024 * 1024
LANES = 128

f32 = jnp.float32
bf16 = jnp.bfloat16
highest = lax.Precision.HIGHEST


def dot(a, b, contract=((1,), (0,)), precision=None):
    return lax.dot_general(
        a, b, (contract, ((), ())), precision=precision, preferred_element_type=f32
    )


ROWS = ((1,), (1,))
COLS = ((0,), (0,))


def split3(v):
    hi = v.astype(bf16)
    rest = v - hi.astype(f32)
    mid = rest.astype(bf16)
    return hi, mid, (rest - mid.astype(f32)).astype(bf16)


def widen(v, expand):
    return dot(jnp.concatenate(split3(v), 1), expand)


def narrow(v, reduce):
    return dot(v.astype(bf16), reduce)


def narrow_exact(v, reduce):
    hi, mid, lo = split3(v)
    return dot(hi, reduce) + dot(mid, reduce) + dot(lo, reduce)


def sigmoid(v):
    return 1.0 / (1.0 + jnp.exp(-v))


def softplus(v):
    return jnp.maximum(v, 0.0) + jnp.log1p(jnp.exp(-jnp.abs(v)))


def conv_forward(pad, match, convp, rows):
    out = convp[4:5, :] + convp[3:4, :] * pad[8 : 8 + rows, :]
    for k in range(3):
        out = out + convp[k : k + 1, :] * pad[5 + k : 5 + k + rows, :] * match[:, k : k + 1]
    return out


def half_masks(rows):
    lane = lax.broadcasted_iota(jnp.int32, (rows, LANES), 1)
    low = jnp.where(lane < LANES // 2, 1.0, 0.0)
    return low.astype(bf16), (1.0 - low).astype(bf16)


def prep_kernel(
    proj, rim, match, convp, headp, expand, xt_o, xs_o, bc_o, cum_o, cumt_o, sin_o, end_o, pref_o,
    thru_o, pad, state, pref,
):
    c = pl.program_id(0)
    rows = proj.shape[0]
    heads = headp.shape[1]

    @pl.when(c == 0)
    def _():
        pad[0:8, :] = rim[...]
        state[...] = jnp.zeros_like(state)
        pref[...] = jnp.ones_like(pref)

    @pl.when(c > 0)
    def _():
        pad[0:8, :] = pad[rows : rows + 8, :]

    pad[8 : 8 + rows, :] = proj[:, DI : DI + XC]
    m = match[...]
    conv = conv_forward(pad, m, convp, rows)
    act = conv * sigmoid(conv)
    dt = softplus(proj[:, DI + XC :] + headp[0:1, :])
    log_decay = dt * headp[1:2, :]
    row = lax.broadcasted_iota(jnp.int32, (rows, rows), 0)
    col = lax.broadcasted_iota(jnp.int32, (rows, rows), 1)
    lower = jnp.where(row >= col, 1.0, 0.0)
    cum = dot(lower, log_decay, precision=highest)
    cum_o[...] = cum
    cumt_o[0] = dot(
        log_decay, jnp.where(row <= col, 1.0, 0.0), COLS, precision=highest
    )
    last = cum[rows - 1 : rows, :]
    wide = widen(
        jnp.concatenate(
            [dt, jnp.exp(last - cum) * m[:, 5:6],
             jnp.broadcast_to(jnp.exp(last) * m[rows - 1 : rows, 4:5], (8, heads))], 0
        ),
        expand[...],
    )
    x = act[:, :DI]
    xt = x * wide[:rows]
    b = act[:, DI : DI + N].astype(bf16)
    xt_o[...] = xt.astype(bf16)
    xs_o[...] = x.astype(bf16)
    bc_o[...] = act[:, DI:].astype(bf16)
    sin_o[0] = state[...].astype(bf16)
    pref_o[0] = pref[...]
    through = wide[2 * rows :]
    state[...] = through[0:1] * state[...] + dot(
        b, (xt * wide[rows : 2 * rows]).astype(bf16), COLS
    )
    pref[...] = pref[...] * through
    end_o[...] = state[...]
    thru_o[...] = pref[...]


def decay_mask(seg_col, seg_row, transposed):
    rows = seg_col.shape[0]
    row = lax.broadcasted_iota(jnp.int32, (rows, rows), 0)
    col = lax.broadcasted_iota(jnp.int32, (rows, rows), 1)
    order = (col >= row) if transposed else (row >= col)
    return (seg_col == seg_row) & order


def intra_kernel(xt, bc, cum, cumt, match, segt, yi_o):
    rows = xt.shape[0]
    mask = decay_mask(match[:, 3:4], segt[0], False)
    scores = dot(bc[:, N:], bc[:, :N], ROWS)
    low, high = half_masks(rows)
    for p in range(xt.shape[1] // LANES):
        mixes = []
        for h in (2 * p, 2 * p + 1):
            gap = cum[:, h : h + 1] - cumt[0, h : h + 1, :]
            mixes.append((jnp.exp(jnp.where(mask, gap, MASKED)) * scores).astype(bf16))
        xp = xt[:, LANES * p : LANES * (p + 1)]
        blocks = jnp.concatenate([xp * low, xp * high], 0)
        yi_o[:, LANES * p : LANES * (p + 1)] = dot(jnp.concatenate(mixes, 1), blocks)


def finish_kernel(
    yi, xs, bc, cum, match, sin_l, pref, dev, z_ref, gains, expand, y_o, no_o, sin_o
):
    sin = (sin_l[0].astype(f32) + pref[0, 0:1, :] * dev[...]).astype(bf16)
    sin_o[0] = sin
    carry = widen(jnp.exp(cum[...]) * match[:, 4:5], expand[...])
    y = yi[...] + carry * dot(bc[:, N:], sin) + gains[1:2, :] * xs[...].astype(f32)
    y_o[...] = y
    z = z_ref[...]
    g = y * z * sigmoid(z)
    r = lax.rsqrt(jnp.mean(g * g, -1, keepdims=True) + EPS)
    no_o[...] = (g * r * gains[0:1, :]).astype(bf16)


def gate_back_kernel(
    gno, y_ref, z_ref, gains, cum, match, bc, pref, expand, dy_o, dz_o, edy_o, og_o, ds_o
):
    @pl.when(pl.program_id(0) == 0)
    def _():
        og_o[...] = jnp.zeros_like(og_o)
        ds_o[...] = jnp.zeros_like(ds_o)

    z = z_ref[...]
    y = y_ref[...]
    sz = sigmoid(z)
    silu = z * sz
    g = y * silu
    r = lax.rsqrt(jnp.mean(g * g, -1, keepdims=True) + EPS)
    gr = g * r
    gv = gno[...]
    og_o[...] += jnp.broadcast_to(jnp.sum(gv * gr, 0, keepdims=True), og_o.shape)
    gn = gv * gains[0:1, :]
    dg = r * (gn - gr * jnp.mean(gn * gr, -1, keepdims=True))
    dy = dg * silu
    dy_o[...] = dy.astype(bf16)
    dz_o[...] = (dg * y * sz * (1.0 + z * (1.0 - sz))).astype(bf16)
    edy = (widen(jnp.exp(cum[...]) * match[:, 4:5], expand[...]) * dy).astype(bf16)
    edy_o[...] = edy
    ds_o[...] += pref[0, 0:1, :] * dot(bc[:, N:], edy, COLS)


def intra_back_kernel(
    dy, xt, bc, cum, cumt, match, segt, reduce, dxi_o, dbc_o, dcum_o, rs
):
    rows = xt.shape[0]
    mask = decay_mask(match[:, 3:4], segt[0], True)
    b = bc[:, :N]
    c = bc[:, N:]
    scores = dot(b, c, ROWS)
    low, high = half_masks(rows)
    rs[...] = jnp.zeros_like(rs)
    dscores = jnp.zeros((rows, rows), f32)
    for p in range(xt.shape[1] // LANES):
        xp = xt[:, LANES * p : LANES * (p + 1)]
        dyp = dy[:, LANES * p : LANES * (p + 1)]
        dmix = dot(jnp.concatenate([xp * low, xp * high], 0), dyp, ROWS)
        mixes = []
        for j in range(2):
            h = 2 * p + j
            gap = cumt[0, h : h + 1, :] - cum[:, h : h + 1]
            decay = jnp.exp(jnp.where(mask, gap, MASKED))
            dm = dmix[rows * j : rows * (j + 1)]
            dscores = dscores + dm * decay
            mix = (decay * scores).astype(bf16)
            mixes.append(mix)
            rs[h : h + 1, :] = jnp.sum(dm * mix.astype(f32), 0, keepdims=True)
        blocks = jnp.concatenate([dyp * low, dyp * high], 0)
        dxi_o[:, LANES * p : LANES * (p + 1)] = dot(jnp.concatenate(mixes, 1), blocks)
    ds = dscores.astype(bf16)
    dbc_o[:, :N] = dot(ds, c)
    dbc_o[:, N:] = dot(ds, b, COLS)
    heads = cum.shape[1]
    cols = narrow_exact(xt[...].astype(f32) * dxi_o[...], reduce[...])
    dcum_o[...] = jnp.transpose(rs[...])[:, :heads] - cols


def sweep_kernel(
    dxi, dbc, dcum, dy, edy, dz, xt, bc, cum, match, sin_ref, proj, before, rim, convp, headp,
    gains, expand, reduce, dsn, gp_o, convg_o, headg_o, rim_o, ds, pad, buf, carry, acc,
):
    i = pl.program_id(0)
    steps = pl.num_programs(0)
    rows = xt.shape[0]
    heads = cum.shape[1]

    @pl.when(i == 0)
    def _():
        ds[...] = dsn[...]
        carry[...] = jnp.zeros_like(carry)
        convg_o[...] = jnp.zeros_like(convg_o)
        headg_o[...] = jnp.zeros_like(headg_o)

    @pl.when(i == steps - 1)
    def _():
        pad[0:8, :] = rim[...]

    @pl.when(i < steps - 1)
    def _():
        pad[0:8, :] = before[:, DI : DI + XC]

    pad[8 : 8 + rows, :] = proj[:, DI : DI + XC]
    m = match[...]
    conv = conv_forward(pad, m, convp, rows)
    sc = sigmoid(conv)
    act = conv * sc
    x = act[:, :DI]
    raw = proj[:, DI + XC :] + headp[0:1, :]
    dt = softplus(raw)
    rate = headp[1:2, :]
    cumv = cum[...]
    last = cumv[rows - 1 : rows, :]
    thru = jnp.exp(last) * m[rows - 1 : rows, 4:5]
    wide = widen(
        jnp.concatenate(
            [dt, jnp.exp(last - cumv) * m[:, 5:6], jnp.broadcast_to(thru, (8, heads))], 0
        ),
        expand[...],
    )
    dt_e = wide[:rows]
    tail_e = wide[rows : 2 * rows]
    thru_e = wide[2 * rows : 2 * rows + 1]
    b = bc[:, :N]
    c = bc[:, N:]
    state_grad = ds[...]
    low_grad = state_grad.astype(bf16)
    sin = sin_ref[0]
    xtv = xt[...].astype(f32)
    dyv = dy[...].astype(f32)
    edyb = edy[...]
    dx_in = tail_e * dot(b, low_grad)
    dxt = dxi[...] + dx_in
    stacked = jnp.concatenate(
        [
            (xtv * dx_in).astype(bf16),
            (edyb.astype(f32) * dot(c, sin)).astype(bf16),
            (x * dxt).astype(bf16),
            (x * dyv).astype(bf16),
        ],
        0,
    )
    sums = dot(stacked, reduce[...])
    db = dbc[:, :N] + dot((tail_e * xtv).astype(bf16), low_grad, ROWS)
    dc = dbc[:, N:] + dot(edyb, sin, ROWS)
    held = jnp.sum(state_grad * sin.astype(f32), 0, keepdims=True)
    dthru = narrow_exact(jnp.broadcast_to(held, (8, held.shape[1])), reduce[...])[0:1] * thru
    ds[...] = thru_e * state_grad + dot(c, edyb, COLS)
    row = lax.broadcasted_iota(jnp.int32, (rows, rows), 0)
    col = lax.broadcasted_iota(jnp.int32, (rows, rows), 1)
    dlog = (
        dot(jnp.where(row <= col, 1.0, 0.0), dcum[...] + sums[rows : 2 * rows], precision=highest)
        + dot(jnp.where(row > col, 1.0, 0.0), sums[:rows], precision=highest)
        + dthru
    )
    ddt = sums[2 * rows : 3 * rows] + dlog * rate
    draw = ddt * sigmoid(raw)
    headg_o[0:1, :] += jnp.sum(draw, 0, keepdims=True)
    headg_o[1:2, :] += jnp.sum(dlog * dt, 0, keepdims=True) * rate
    headg_o[2:3, :] += jnp.sum(sums[3 * rows :], 0, keepdims=True)
    gp_o[:, :DI] = dz[...]
    gp_o[:, DI + XC :] = draw.astype(bf16)
    dact = jnp.concatenate([dt_e * dxt + gains[1:2, :] * dyv, db, dc], 1)
    dconv = dact * (sc * (1.0 + conv * (1.0 - sc)))
    convg_o[4:5, :] += jnp.sum(dconv, 0, keepdims=True)
    convg_o[3:4, :] += jnp.sum(dconv * pad[8 : 8 + rows, :], 0, keepdims=True)
    acc[...] = dconv * convp[3:4, :]
    rim_sum = jnp.zeros((8, XC), f32)
    for k in range(3):
        v = dconv * m[:, k : k + 1]
        convg_o[k : k + 1, :] += jnp.sum(v * pad[5 + k : 5 + k + rows, :], 0, keepdims=True)
        v = v * convp[k : k + 1, :]
        buf[0:8, :] = jnp.zeros((8, XC), f32)
        buf[8 : 8 + rows, :] = v
        buf[8 + rows : 16 + rows, :] = carry[8 * k : 8 * k + 8, :]
        shift = 3 - k
        acc[...] += buf[8 + shift : 8 + shift + rows, :]
        rim_sum = rim_sum + buf[shift : 8 + shift, :]
        carry[8 * k : 8 * k + 8, :] = v[0:8, :]
    gp_o[:, DI : DI + XC] = acc[...].astype(bf16)
    rim_o[...] = rim_sum


def shapes(*specs):
    return [jax.ShapeDtypeStruct(s, d) for s, d in specs]


def by_chunk(rows, cols, steps=None):
    if steps is None:
        return pl.BlockSpec((rows, cols), lambda i: (i, 0))
    return pl.BlockSpec((rows, cols), lambda i: (steps - 1 - i, 0))


def by_lead(a, b, steps=None):
    if steps is None:
        return pl.BlockSpec((1, a, b), lambda i: (i, 0, 0))
    return pl.BlockSpec((1, a, b), lambda i: (steps - 1 - i, 0, 0))


def fixed(*shape):
    return pl.BlockSpec(shape, lambda i: (0,) * len(shape))


def call(kernel, steps, ins, outs, out_shape, scratch=(), flops=0, moved=0):
    return pl.pallas_call(
        kernel,
        grid=(steps,),
        in_specs=ins,
        out_specs=outs,
        out_shape=out_shape,
        scratch_shapes=scratch,
        compiler_params=pltpu.CompilerParams(
            dimension_semantics=("arbitrary",), vmem_limit_bytes=VMEM_LIMIT
        ),
        cost_estimate=pl.CostEstimate(flops=flops, bytes_accessed=moved, transcendentals=0),
    )


def shifted(value, axis, steps):
    count = lax.axis_size(axis)
    initial, last = (max(0, -steps), min(count, count - steps))
    return lax.ppermute(value, axis, [(source, source + steps) for source in range(initial, last)])


def relay(through, local, steps):
    incoming = shifted(local, "seq", steps)
    for _ in range(lax.axis_size("seq") - 2):
        incoming = shifted(through[0:1] * incoming + local, "seq", steps)
    return incoming


def rms_scale(values, gain):
    return values * lax.rsqrt(jnp.mean(values * values, -1, keepdims=True) + EPS) * gain


def layer_forward(source, w, seg):
    match, segt, rows = seg["match"], seg["segt"], seg["rows"]
    T = source.shape[0]
    nc = T // rows
    H = w["headp"].shape[1]
    PWL = w["win"].shape[1]
    normed = rms_scale(source, w["norm_gain"]).astype(bf16)
    proj = dot(normed, w["win"])
    rim = shifted(proj[-8:, DI : DI + XC], "seq", 1)
    expand = seg["expand"]
    xt, xs, bc, cum, cumt, sin_l, end, pref, thru = call(
        prep_kernel,
        nc,
        [by_chunk(rows, PWL), fixed(8, XC), by_chunk(rows, 8), fixed(8, XC), fixed(8, H),
         fixed(*expand.shape)],
        [by_chunk(rows, DI), by_chunk(rows, DI), by_chunk(rows, 2 * N), by_chunk(rows, H),
         by_lead(H, rows), by_lead(N, DI), fixed(N, DI), by_lead(8, DI), fixed(8, DI)],
        shapes(((T, DI), bf16), ((T, DI), bf16), ((T, 2 * N), bf16), ((T, H), f32),
               ((nc, H, rows), f32), ((nc, N, DI), bf16), ((N, DI), f32), ((nc, 8, DI), f32),
               ((8, DI), f32)),
        [pltpu.VMEM((rows + 8, XC), f32), pltpu.VMEM((N, DI), f32), pltpu.VMEM((8, DI), f32)],
        flops=int(2e9), moved=int(1.5e7),
    )(proj, rim, match, w["convp"], w["headp"], expand)
    dev = relay(thru, end, 1)
    yi = call(
        intra_kernel,
        nc,
        [by_chunk(rows, DI), by_chunk(rows, 2 * N), by_chunk(rows, H), by_lead(H, rows),
         by_chunk(rows, 8), by_lead(1, rows)],
        by_chunk(rows, DI),
        jax.ShapeDtypeStruct((T, DI), f32),
        flops=int(8e9), moved=int(5e6),
    )(xt, bc, cum, cumt, match, segt)
    y, normed_out, sin = call(
        finish_kernel,
        nc,
        [by_chunk(rows, DI), by_chunk(rows, DI), by_chunk(rows, 2 * N), by_chunk(rows, H),
         by_chunk(rows, 8), by_lead(N, DI), by_lead(8, DI), fixed(N, DI), by_chunk(rows, DI),
         fixed(8, DI), fixed(*expand.shape)],
        [by_chunk(rows, DI), by_chunk(rows, DI), by_lead(N, DI)],
        shapes(((T, DI), f32), ((T, DI), bf16), ((nc, N, DI), bf16)),
        flops=int(2e9), moved=int(1.5e7),
    )(yi, xs, bc, cum, match, sin_l, pref, dev, proj, w["gains"], expand)
    out = source + dot(normed_out, w["wout"])
    kept = dict(
        source=source, normed=normed, proj=proj, rim=rim, xt=xt, bc=bc, cum=cum, cumt=cumt,
        pref=pref, thru=thru, y=y, normed_out=normed_out, sin=sin,
    )
    return out, kept


def layer_backward(grad_low, w, seg, kept):
    match, segt, rows = seg["match"], seg["segt"], seg["rows"]
    T = grad_low.shape[0]
    nc = T // rows
    H = w["headp"].shape[1]
    PWL = w["win"].shape[1]
    expand, reduce = seg["expand"], seg["reduce"]
    proj, bc, cum, xt = kept["proj"], kept["bc"], kept["cum"], kept["xt"]
    gno = dot(grad_low, w["wout"], ROWS)
    dy, dz, edy, og, ds_local = call(
        gate_back_kernel,
        nc,
        [by_chunk(rows, DI), by_chunk(rows, DI), by_chunk(rows, DI), fixed(8, DI),
         by_chunk(rows, H), by_chunk(rows, 8), by_chunk(rows, 2 * N), by_lead(8, DI),
         fixed(*expand.shape)],
        [by_chunk(rows, DI), by_chunk(rows, DI), by_chunk(rows, DI), fixed(8, DI), fixed(N, DI)],
        shapes(((T, DI), bf16), ((T, DI), bf16), ((T, DI), bf16), ((8, DI), f32), ((N, DI), f32)),
        flops=int(2e9), moved=int(1.5e7),
    )(gno, kept["y"], proj, w["gains"], cum, match, bc, kept["pref"], expand)
    dsn = relay(kept["thru"], ds_local, -1)
    dxi, dbc, dcum = call(
        intra_back_kernel,
        nc,
        [by_chunk(rows, DI), by_chunk(rows, DI), by_chunk(rows, 2 * N), by_chunk(rows, H),
         by_lead(H, rows), by_chunk(rows, 8), by_lead(1, rows), fixed(*reduce.shape)],
        [by_chunk(rows, DI), by_chunk(rows, 2 * N), by_chunk(rows, H)],
        shapes(((T, DI), f32), ((T, 2 * N), f32), ((T, H), f32)),
        [pltpu.VMEM((LANES, rows), f32)],
        flops=int(2e10), moved=int(1e7),
    )(dy, xt, bc, cum, kept["cumt"], match, segt, reduce)
    rc = functools_rev(rows, nc)
    gp, convg, headg, rim_grad = call(
        sweep_kernel,
        nc,
        [rc(DI), rc(2 * N), rc(H), rc(DI), rc(DI), rc(DI), rc(DI), rc(2 * N), rc(H), rc(8),
         by_lead(N, DI, nc), rc(PWL),
         pl.BlockSpec((8, PWL), lambda i: (jnp.maximum((nc - 1 - i) * (rows // 8) - 1, 0), 0)),
         fixed(8, XC), fixed(8, XC), fixed(8, H), fixed(8, DI), fixed(*expand.shape),
         fixed(*reduce.shape), fixed(N, DI)],
        [rc(PWL), fixed(8, XC), fixed(8, H), fixed(8, XC)],
        shapes(((T, PWL), bf16), ((8, XC), f32), ((8, H), f32), ((8, XC), f32)),
        [pltpu.VMEM((N, DI), f32), pltpu.VMEM((rows + 8, XC), f32),
         pltpu.VMEM((rows + 16, XC), f32), pltpu.VMEM((24, XC), f32),
         pltpu.VMEM((rows, XC), f32)],
        flops=int(4e9), moved=int(2e7),
    )(dxi, dbc, dcum, dy, edy, dz, xt, bc, cum, match, kept["sin"], proj, proj, kept["rim"],
      w["convp"], w["headp"], w["gains"], expand, reduce, dsn)
    returned = shifted(rim_grad, "seq", -1)
    tail = (gp[-16:, DI : DI + XC].astype(f32)
            + jnp.concatenate([jnp.zeros_like(returned), returned], 0)).astype(bf16)
    gp = lax.dynamic_update_slice(gp, tail, (T - 16, DI))
    grad_normed = dot(gp, w["win"], ROWS)
    _, norm_pull = jax.vjp(rms_scale, kept["source"], w["norm_gain"])
    grad_source, grad_norm_gain = norm_pull(grad_normed)
    grad_in = dot(kept["normed"], gp, COLS)
    grad_out = dot(kept["normed_out"], grad_low, COLS)
    return grad_source, (grad_in, grad_out, grad_norm_gain, convg, og[0], headg)


def functools_rev(rows, nc):
    return lambda cols: by_chunk(rows, cols, nc)


def seg_tables(segments, rows, heads):
    T = segments.shape[0]
    seg = segments.astype(f32)
    rim = shifted(seg[-3:], "seq", 1)
    padded = jnp.concatenate([rim, seg])
    cols = [(padded[k : k + T] == seg).astype(f32) for k in range(3)]
    chunked = seg.reshape(-1, rows)
    ends = chunked[:, -1]
    starts = jnp.concatenate([rim[-1:], ends[:-1]])
    cols.append(seg)
    cols.append((chunked == starts[:, None]).astype(f32).reshape(-1))
    cols.append((chunked == ends[:, None]).astype(f32).reshape(-1))
    match = jnp.stack(cols + [jnp.zeros_like(seg)] * 2, 1)
    head_of = jnp.arange(DI) // (DI // heads)
    one = (jnp.arange(heads)[:, None] == head_of[None, :]).astype(bf16)
    return dict(
        match=match, segt=chunked[:, None, :], rows=rows,
        expand=jnp.concatenate([one, one, one], 0), reduce=one.T,
    )


def shards(
    tokens, cotangent, segments, norm_gain, in_weight, conv_weight, conv_bias, dt_bias, decay_log,
    skip_gain, out_gain, out_weight,
):
    section = lax.axis_index("section")
    is_first = section == 0
    D = tokens.shape[-1]
    H = dt_bias.shape[-1]
    T = tokens.shape[2]
    rows = min(LANES, T)
    cut = conv_weight.shape[-1]
    everyone = ("section", "seq", "dp")
    mine = partial(lax.dynamic_index_in_dim, index=section, axis=0, keepdims=False)
    source = mine(tokens)[0]
    grad_low = mine(cotangent)[0]
    seg = seg_tables(mine(segments)[0], rows, H)

    small = jnp.concatenate(
        [norm_gain[0], conv_weight[0].reshape(-1), conv_bias[0], out_gain[0]]
    )[None]
    small = lax.all_gather(small, everyone, axis=0, tiled=True)
    small = small.reshape(2, -1, small.shape[-1]).astype(f32)
    heads_own = jnp.concatenate([dt_bias, -jnp.exp(decay_log), skip_gain], 0)
    heads_other = lax.ppermute(heads_own, "section", [(0, 1), (1, 0)])
    win = lax.all_gather(in_weight, everyone, axis=1, tiled=True).reshape(2, D, -1)
    wout = lax.all_gather(out_weight, everyone, axis=1, tiled=True).reshape(2, DI, D)
    weights = []
    nd, no = norm_gain.shape[-1], out_gain.shape[-1]
    for s in range(2):
        vec = small[s]
        heads = jnp.where(section == s, heads_own, heads_other)
        taps = vec[:, nd : nd + 4 * cut].reshape(-1, 4, cut)
        taps = jnp.swapaxes(taps, 0, 1).reshape(4, -1)
        bias = vec[:, nd + 4 * cut : nd + 5 * cut].reshape(1, -1)
        gain = vec[:, nd + 5 * cut :].reshape(1, -1)
        skip = jnp.repeat(heads[2], DI // H)[None]
        weights.append(dict(
            norm_gain=vec[:, :nd].reshape(-1),
            convp=jnp.concatenate([taps, bias, jnp.zeros((3, XC), f32)], 0),
            headp=jnp.concatenate([heads, jnp.zeros((5, H), f32)], 0),
            gains=jnp.concatenate([gain, skip, jnp.zeros((6, DI), f32)], 0),
            win=win[s], wout=wout[s],
        ))

    swap = [(0, 1), (1, 0)]
    out0, kept0 = layer_forward(source.astype(f32), weights[0], seg)
    passed = out0.astype(bf16)
    out1, kept1 = layer_forward(passed.astype(f32), weights[1], seg)
    final = out1.astype(bf16)
    got = lax.ppermute(jnp.where(is_first, final, passed), "section", swap)
    own = jnp.where(is_first, passed, final)
    section_outputs = jnp.where(is_first, jnp.stack([own, got]), jnp.stack([got, own]))

    grad1, terms1 = layer_backward(grad_low, weights[1], seg, kept1)
    middle = (grad_low.astype(f32) + grad1).astype(bf16)
    grad0, terms0 = layer_backward(middle, weights[0], seg, kept0)
    first = middle.astype(f32) + grad0
    got = lax.ppermute(jnp.where(is_first, middle, first.astype(bf16)), "section", swap)
    got = got.astype(f32)
    own = jnp.where(is_first, first, middle.astype(f32))
    input_grads = jnp.where(is_first, jnp.stack([own, got]), jnp.stack([got, own]))

    def both(position):
        return jnp.stack([terms0[position], terms1[position]])

    def scatter(value, axis):
        return lax.psum_scatter(value, everyone, scatter_dimension=axis, tiled=True)

    grad_in = scatter(both(0).astype(bf16).reshape(2 * D, -1), 0).astype(f32)[None]
    grad_out = scatter(both(1).astype(bf16).reshape(2 * DI, -1), 0).astype(f32)[None]
    convg = both(3)
    packed = jnp.concatenate(
        [both(2).reshape(2, -1, nd),
         jnp.swapaxes(convg[:, :4].reshape(2, 4, -1, cut), 1, 2).reshape(2, -1, 4 * cut),
         convg[:, 4].reshape(2, -1, cut), both(4).reshape(2, -1, no)], -1
    )
    vec = scatter(packed.reshape(-1, packed.shape[-1]), 0)[0]
    head_sums = lax.psum(both(5)[:, :3], everyone)
    head_sums = jnp.where(is_first, head_sums[0], head_sums[1])
    return (
        section_outputs[None, :, None],
        input_grads[None, :, None],
        vec[None, :nd],
        grad_in,
        vec[nd : nd + 4 * cut].reshape(1, 4, cut),
        vec[None, nd + 4 * cut : nd + 5 * cut],
        head_sums[0:1],
        head_sums[1:2],
        head_sums[2:3],
        vec[None, nd + 5 * cut :],
        grad_out,
    )


def solution(mesh):
    placed = (
        P(None, "dp", "seq", None),
        P(None, "dp", "seq", None),
        P(None, "dp", "seq"),
        P("section", ("seq", "dp")),
        P("section", ("seq", "dp"), None),
        P("section", None, ("seq", "dp")),
        P("section", ("seq", "dp")),
        P("section", None),
        P("section", None),
        P("section", None),
        P("section", ("seq", "dp")),
        P("section", ("seq", "dp"), None),
    )
    return jax.shard_map(
        shards,
        mesh=mesh,
        in_specs=placed,
        out_specs=(
            P("section", None, "dp", "seq", None),
            P("section", None, "dp", "seq", None),
            P("section", ("seq", "dp")),
            P("section", ("seq", "dp"), None),
            P("section", None, ("seq", "dp")),
            P("section", ("seq", "dp")),
            P("section", None),
            P("section", None),
            P("section", None),
            P("section", ("seq", "dp")),
            P("section", ("seq", "dp"), None),
        ),
        check_vma=False,
    )
```

```python
from functools import partial

import jax
import jax.numpy as jnp
from jax import lax
from jax.experimental import pallas as pl
from jax.experimental.pallas import tpu as pltpu
from jax.sharding import PartitionSpec as P

DI = 1536
N = 128
XC = 1792
EPS = 1e-05
MASKED = -1e30
VMEM_LIMIT = 40 * 1024 * 1024
LANES = 128

f32 = jnp.float32
bf16 = jnp.bfloat16
highest = lax.Precision.HIGHEST


def dot(a, b, contract=((1,), (0,)), precision=None):
    return lax.dot_general(
        a, b, (contract, ((), ())), precision=precision, preferred_element_type=f32
    )


ROWS = ((1,), (1,))
COLS = ((0,), (0,))


def split3(v):
    hi = v.astype(bf16)
    rest = v - hi.astype(f32)
    mid = rest.astype(bf16)
    return hi, mid, (rest - mid.astype(f32)).astype(bf16)


def widen(v, expand):
    return dot(jnp.concatenate(split3(v), 1), expand)


def narrow(v, reduce):
    return dot(v.astype(bf16), reduce)


def narrow_exact(v, reduce):
    hi, mid, lo = split3(v)
    return dot(hi, reduce) + dot(mid, reduce) + dot(lo, reduce)


def sigmoid(v):
    return 1.0 / (1.0 + jnp.exp(-v))


def softplus(v):
    return jnp.maximum(v, 0.0) + jnp.log1p(jnp.exp(-jnp.abs(v)))


def conv_forward(pad, match, convp, rows):
    out = convp[4:5, :] + convp[3:4, :] * pad[8 : 8 + rows, :]
    for k in range(3):
        out = out + convp[k : k + 1, :] * pad[5 + k : 5 + k + rows, :] * match[:, k : k + 1]
    return out


def half_masks(rows):
    lane = lax.broadcasted_iota(jnp.int32, (rows, LANES), 1)
    low = jnp.where(lane < LANES // 2, 1.0, 0.0)
    return low.astype(bf16), (1.0 - low).astype(bf16)


def prep_kernel(
    proj, rim, match, convp, headp, expand, xt_o, xs_o, bc_o, cum_o, cumt_o, sin_o, end_o, pref_o,
    thru_o, pad, state, pref,
):
    c = pl.program_id(0)
    rows = proj.shape[0]
    heads = headp.shape[1]

    @pl.when(c == 0)
    def _():
        pad[0:8, :] = rim[...]
        state[...] = jnp.zeros_like(state)
        pref[...] = jnp.ones_like(pref)

    @pl.when(c > 0)
    def _():
        pad[0:8, :] = pad[rows : rows + 8, :]

    pad[8 : 8 + rows, :] = proj[:, DI : DI + XC]
    m = match[...]
    conv = conv_forward(pad, m, convp, rows)
    act = conv * sigmoid(conv)
    dt = softplus(proj[:, DI + XC : DI + XC + heads] + headp[0:1, :])
    log_decay = dt * headp[1:2, :]
    row = lax.broadcasted_iota(jnp.int32, (rows, rows), 0)
    col = lax.broadcasted_iota(jnp.int32, (rows, rows), 1)
    lower = jnp.where(row >= col, 1.0, 0.0)
    cum = dot(lower, log_decay, precision=highest)
    cum_o[...] = cum
    cumt_o[0] = dot(
        log_decay, jnp.where(row <= col, 1.0, 0.0), COLS, precision=highest
    )
    last = cum[rows - 1 : rows, :]
    wide = widen(
        jnp.concatenate(
            [dt, jnp.exp(last - cum) * m[:, 5:6],
             jnp.broadcast_to(jnp.exp(last) * m[rows - 1 : rows, 4:5], (8, heads))], 0
        ),
        expand[...],
    )
    x = act[:, :DI]
    xt = x * wide[:rows]
    b = act[:, DI : DI + N].astype(bf16)
    xt_o[...] = xt.astype(bf16)
    xs_o[...] = x.astype(bf16)
    bc_o[...] = act[:, DI:].astype(bf16)
    sin_o[0] = state[...].astype(bf16)
    pref_o[0] = pref[...]
    through = wide[2 * rows :]
    state[...] = through[0:1] * state[...] + dot(
        b, (xt * wide[rows : 2 * rows]).astype(bf16), COLS
    )
    pref[...] = pref[...] * through
    end_o[...] = state[...]
    thru_o[...] = pref[...]


def decay_mask(seg_col, seg_row, transposed):
    rows = seg_col.shape[0]
    row = lax.broadcasted_iota(jnp.int32, (rows, rows), 0)
    col = lax.broadcasted_iota(jnp.int32, (rows, rows), 1)
    order = (col >= row) if transposed else (row >= col)
    return (seg_col == seg_row) & order


def intra_kernel(xt, bc, cum, cumt, match, segt, yi_o):
    rows = xt.shape[0]
    mask = decay_mask(match[:, 3:4], segt[0], False)
    scores = dot(bc[:, N:], bc[:, :N], ROWS)
    low, high = half_masks(rows)
    for p in range(xt.shape[1] // LANES):
        mixes = []
        for h in (2 * p, 2 * p + 1):
            gap = cum[:, h : h + 1] - cumt[0, h : h + 1, :]
            mixes.append((jnp.exp(jnp.where(mask, gap, MASKED)) * scores).astype(bf16))
        xp = xt[:, LANES * p : LANES * (p + 1)]
        blocks = jnp.concatenate([xp * low, xp * high], 0)
        yi_o[:, LANES * p : LANES * (p + 1)] = dot(jnp.concatenate(mixes, 1), blocks)


def finish_kernel(
    yi, xs, bc, cum, match, sin_l, pref, dev, z_ref, gains, expand, y_o, no_o, sin_o
):
    sin = (sin_l[0].astype(f32) + pref[0, 0:1, :] * dev[...]).astype(bf16)
    sin_o[0] = sin
    carry = widen(jnp.exp(cum[...]) * match[:, 4:5], expand[...])
    y = yi[...] + carry * dot(bc[:, N:], sin) + gains[1:2, :] * xs[...].astype(f32)
    y_o[...] = y
    z = z_ref[...]
    g = y * z * sigmoid(z)
    r = lax.rsqrt(jnp.mean(g * g, -1, keepdims=True) + EPS)
    no_o[...] = (g * r * gains[0:1, :]).astype(bf16)


def gate_back_kernel(
    gno, y_ref, z_ref, gains, cum, match, bc, pref, expand, dy_o, dz_o, edy_o, og_o, ds_o
):
    @pl.when(pl.program_id(0) == 0)
    def _():
        og_o[...] = jnp.zeros_like(og_o)
        ds_o[...] = jnp.zeros_like(ds_o)

    z = z_ref[...]
    y = y_ref[...]
    sz = sigmoid(z)
    silu = z * sz
    g = y * silu
    r = lax.rsqrt(jnp.mean(g * g, -1, keepdims=True) + EPS)
    gr = g * r
    gv = gno[...]
    og_o[...] += jnp.broadcast_to(jnp.sum(gv * gr, 0, keepdims=True), og_o.shape)
    gn = gv * gains[0:1, :]
    dg = r * (gn - gr * jnp.mean(gn * gr, -1, keepdims=True))
    dy = dg * silu
    dy_o[...] = dy.astype(bf16)
    dz_o[...] = (dg * y * sz * (1.0 + z * (1.0 - sz))).astype(bf16)
    edy = (widen(jnp.exp(cum[...]) * match[:, 4:5], expand[...]) * dy).astype(bf16)
    edy_o[...] = edy
    ds_o[...] += pref[0, 0:1, :] * dot(bc[:, N:], edy, COLS)


def intra_back_kernel(
    dy, xt, bc, cum, cumt, match, segt, reduce, dxi_o, dbc_o, dcum_o, rs
):
    rows = xt.shape[0]
    mask = decay_mask(match[:, 3:4], segt[0], True)
    b = bc[:, :N]
    c = bc[:, N:]
    scores = dot(b, c, ROWS)
    low, high = half_masks(rows)
    rs[...] = jnp.zeros_like(rs)
    dscores = jnp.zeros((rows, rows), f32)
    for p in range(xt.shape[1] // LANES):
        xp = xt[:, LANES * p : LANES * (p + 1)]
        dyp = dy[:, LANES * p : LANES * (p + 1)]
        dmix = dot(jnp.concatenate([xp * low, xp * high], 0), dyp, ROWS)
        mixes = []
        for j in range(2):
            h = 2 * p + j
            gap = cumt[0, h : h + 1, :] - cum[:, h : h + 1]
            decay = jnp.exp(jnp.where(mask, gap, MASKED))
            dm = dmix[rows * j : rows * (j + 1)]
            dscores = dscores + dm * decay
            mix = (decay * scores).astype(bf16)
            mixes.append(mix)
            rs[h : h + 1, :] = jnp.sum(dm * mix.astype(f32), 0, keepdims=True)
        blocks = jnp.concatenate([dyp * low, dyp * high], 0)
        dxi_o[:, LANES * p : LANES * (p + 1)] = dot(jnp.concatenate(mixes, 1), blocks)
    ds = dscores.astype(bf16)
    dbc_o[:, :N] = dot(ds, c)
    dbc_o[:, N:] = dot(ds, b, COLS)
    heads = cum.shape[1]
    cols = narrow_exact(xt[...].astype(f32) * dxi_o[...], reduce[...])
    dcum_o[...] = jnp.transpose(rs[...])[:, :heads] - cols


def sweep_kernel(
    dxi, dbc, dcum, dy, edy, dz, xt, bc, cum, match, sin_ref, proj, before, rim, convp, headp,
    gains, expand, reduce, dsn, gp_o, convg_o, headg_o, rim_o, ds, pad, buf, carry, acc,
):
    i = pl.program_id(0)
    steps = pl.num_programs(0)
    rows = xt.shape[0]
    heads = cum.shape[1]

    @pl.when(i == 0)
    def _():
        ds[...] = dsn[...]
        carry[...] = jnp.zeros_like(carry)
        convg_o[...] = jnp.zeros_like(convg_o)
        headg_o[...] = jnp.zeros_like(headg_o)

    @pl.when(i == steps - 1)
    def _():
        pad[0:8, :] = rim[...]

    @pl.when(i < steps - 1)
    def _():
        pad[0:8, :] = before[:, DI : DI + XC]

    pad[8 : 8 + rows, :] = proj[:, DI : DI + XC]
    m = match[...]
    conv = conv_forward(pad, m, convp, rows)
    sc = sigmoid(conv)
    act = conv * sc
    x = act[:, :DI]
    raw = proj[:, DI + XC : DI + XC + heads] + headp[0:1, :]
    dt = softplus(raw)
    rate = headp[1:2, :]
    cumv = cum[...]
    last = cumv[rows - 1 : rows, :]
    thru = jnp.exp(last) * m[rows - 1 : rows, 4:5]
    wide = widen(
        jnp.concatenate(
            [dt, jnp.exp(last - cumv) * m[:, 5:6], jnp.broadcast_to(thru, (8, heads))], 0
        ),
        expand[...],
    )
    dt_e = wide[:rows]
    tail_e = wide[rows : 2 * rows]
    thru_e = wide[2 * rows : 2 * rows + 1]
    b = bc[:, :N]
    c = bc[:, N:]
    state_grad = ds[...]
    low_grad = state_grad.astype(bf16)
    sin = sin_ref[0]
    xtv = xt[...].astype(f32)
    dyv = dy[...].astype(f32)
    edyb = edy[...]
    dx_in = tail_e * dot(b, low_grad)
    dxt = dxi[...] + dx_in
    stacked = jnp.concatenate(
        [
            (xtv * dx_in).astype(bf16),
            (edyb.astype(f32) * dot(c, sin)).astype(bf16),
            (x * dxt).astype(bf16),
            (x * dyv).astype(bf16),
        ],
        0,
    )
    sums = dot(stacked, reduce[...])
    db = dbc[:, :N] + dot((tail_e * xtv).astype(bf16), low_grad, ROWS)
    dc = dbc[:, N:] + dot(edyb, sin, ROWS)
    held = jnp.sum(state_grad * sin.astype(f32), 0, keepdims=True)
    dthru = narrow_exact(jnp.broadcast_to(held, (8, held.shape[1])), reduce[...])[0:1] * thru
    ds[...] = thru_e * state_grad + dot(c, edyb, COLS)
    row = lax.broadcasted_iota(jnp.int32, (rows, rows), 0)
    col = lax.broadcasted_iota(jnp.int32, (rows, rows), 1)
    dlog = (
        dot(jnp.where(row <= col, 1.0, 0.0), dcum[...] + sums[rows : 2 * rows], precision=highest)
        + dot(jnp.where(row > col, 1.0, 0.0), sums[:rows], precision=highest)
        + dthru
    )
    ddt = sums[2 * rows : 3 * rows] + dlog * rate
    draw = ddt * sigmoid(raw)
    headg_o[0:1, :] += jnp.sum(draw, 0, keepdims=True)
    headg_o[1:2, :] += jnp.sum(dlog * dt, 0, keepdims=True) * rate
    headg_o[2:3, :] += jnp.sum(sums[3 * rows :], 0, keepdims=True)
    gp_o[:, :DI] = dz[...]
    gp_o[:, DI + XC :] = jnp.zeros((rows, gp_o.shape[1] - DI - XC), bf16)
    gp_o[:, DI + XC : DI + XC + heads] = draw.astype(bf16)
    dact = jnp.concatenate([dt_e * dxt + gains[1:2, :] * dyv, db, dc], 1)
    dconv = dact * (sc * (1.0 + conv * (1.0 - sc)))
    convg_o[4:5, :] += jnp.sum(dconv, 0, keepdims=True)
    convg_o[3:4, :] += jnp.sum(dconv * pad[8 : 8 + rows, :], 0, keepdims=True)
    acc[...] = dconv * convp[3:4, :]
    rim_sum = jnp.zeros((8, XC), f32)
    for k in range(3):
        v = dconv * m[:, k : k + 1]
        convg_o[k : k + 1, :] += jnp.sum(v * pad[5 + k : 5 + k + rows, :], 0, keepdims=True)
        v = v * convp[k : k + 1, :]
        buf[0:8, :] = jnp.zeros((8, XC), f32)
        buf[8 : 8 + rows, :] = v
        buf[8 + rows : 16 + rows, :] = carry[8 * k : 8 * k + 8, :]
        shift = 3 - k
        acc[...] += buf[8 + shift : 8 + shift + rows, :]
        rim_sum = rim_sum + buf[shift : 8 + shift, :]
        carry[8 * k : 8 * k + 8, :] = v[0:8, :]
    gp_o[:, DI : DI + XC] = acc[...].astype(bf16)
    rim_o[...] = rim_sum


def shapes(*specs):
    return [jax.ShapeDtypeStruct(s, d) for s, d in specs]


def by_chunk(rows, cols, steps=None):
    if steps is None:
        return pl.BlockSpec((rows, cols), lambda i: (i, 0))
    return pl.BlockSpec((rows, cols), lambda i: (steps - 1 - i, 0))


def by_lead(a, b, steps=None):
    if steps is None:
        return pl.BlockSpec((1, a, b), lambda i: (i, 0, 0))
    return pl.BlockSpec((1, a, b), lambda i: (steps - 1 - i, 0, 0))


def fixed(*shape):
    return pl.BlockSpec(shape, lambda i: (0,) * len(shape))


def call(kernel, steps, ins, outs, out_shape, scratch=()):
    return pl.pallas_call(
        kernel,
        grid=(steps,),
        in_specs=ins,
        out_specs=outs,
        out_shape=out_shape,
        scratch_shapes=scratch,
        compiler_params=pltpu.CompilerParams(
            dimension_semantics=("arbitrary",), vmem_limit_bytes=VMEM_LIMIT
        ),
        cost_estimate=pl.CostEstimate(flops=1000, bytes_accessed=1000, transcendentals=0),
    )


def shifted(value, axis, steps):
    count = lax.axis_size(axis)
    initial, last = (max(0, -steps), min(count, count - steps))
    return lax.ppermute(value, axis, [(source, source + steps) for source in range(initial, last)])


def relay(through, local, steps):
    incoming = shifted(local, "seq", steps)
    for _ in range(lax.axis_size("seq") - 2):
        incoming = shifted(through[0:1] * incoming + local, "seq", steps)
    return incoming


def rms_scale(values, gain):
    return values * lax.rsqrt(jnp.mean(values * values, -1, keepdims=True) + EPS) * gain


def layer_forward(source, w, seg):
    match, segt, rows = seg["match"], seg["segt"], seg["rows"]
    T = source.shape[0]
    nc = T // rows
    H = w["headp"].shape[1]
    PWL = w["win"].shape[1]
    normed = rms_scale(source, w["norm_gain"]).astype(bf16)
    proj = dot(normed, w["win"])
    rim = shifted(proj[-8:, DI : DI + XC], "seq", 1)
    expand = seg["expand"]
    xt, xs, bc, cum, cumt, sin_l, end, pref, thru = call(
        prep_kernel,
        nc,
        [by_chunk(rows, PWL), fixed(8, XC), by_chunk(rows, 8), fixed(8, XC), fixed(8, H),
         fixed(*expand.shape)],
        [by_chunk(rows, DI), by_chunk(rows, DI), by_chunk(rows, 2 * N), by_chunk(rows, H),
         by_lead(H, rows), by_lead(N, DI), fixed(N, DI), by_lead(8, DI), fixed(8, DI)],
        shapes(((T, DI), bf16), ((T, DI), bf16), ((T, 2 * N), bf16), ((T, H), f32),
               ((nc, H, rows), f32), ((nc, N, DI), bf16), ((N, DI), f32), ((nc, 8, DI), f32),
               ((8, DI), f32)),
        [pltpu.VMEM((rows + 8, XC), f32), pltpu.VMEM((N, DI), f32), pltpu.VMEM((8, DI), f32)],
    )(proj, rim, match, w["convp"], w["headp"], expand)
    dev = relay(thru, end, 1)
    yi = call(
        intra_kernel,
        nc,
        [by_chunk(rows, DI), by_chunk(rows, 2 * N), by_chunk(rows, H), by_lead(H, rows),
         by_chunk(rows, 8), by_lead(1, rows)],
        by_chunk(rows, DI),
        jax.ShapeDtypeStruct((T, DI), f32),
    )(xt, bc, cum, cumt, match, segt)
    y, normed_out, sin = call(
        finish_kernel,
        nc,
        [by_chunk(rows, DI), by_chunk(rows, DI), by_chunk(rows, 2 * N), by_chunk(rows, H),
         by_chunk(rows, 8), by_lead(N, DI), by_lead(8, DI), fixed(N, DI), by_chunk(rows, DI),
         fixed(8, DI), fixed(*expand.shape)],
        [by_chunk(rows, DI), by_chunk(rows, DI), by_lead(N, DI)],
        shapes(((T, DI), f32), ((T, DI), bf16), ((nc, N, DI), bf16)),
    )(yi, xs, bc, cum, match, sin_l, pref, dev, proj, w["gains"], expand)
    out = source + dot(normed_out, w["wout"])
    kept = dict(
        source=source, normed=normed, proj=proj, rim=rim, xt=xt, bc=bc, cum=cum, cumt=cumt,
        pref=pref, thru=thru, y=y, normed_out=normed_out, sin=sin,
    )
    return out, kept


def layer_backward(grad_low, w, seg, kept, beside):
    match, segt, rows = seg["match"], seg["segt"], seg["rows"]
    T = grad_low.shape[0]
    nc = T // rows
    H = w["headp"].shape[1]
    PWL = w["win"].shape[1]
    expand, reduce = seg["expand"], seg["reduce"]
    proj, bc, cum, xt = kept["proj"], kept["bc"], kept["cum"], kept["xt"]
    grad_low = move(beside, grad_low)
    out_sums, grad_low = fold([kept["normed_out"]], lambda g: [g], grad_low)
    gno = dot(grad_low, w["wout"], ROWS)
    dy, dz, edy, og, ds_local = call(
        gate_back_kernel,
        nc,
        [by_chunk(rows, DI), by_chunk(rows, DI), by_chunk(rows, DI), fixed(8, DI),
         by_chunk(rows, H), by_chunk(rows, 8), by_chunk(rows, 2 * N), by_lead(8, DI),
         fixed(*expand.shape)],
        [by_chunk(rows, DI), by_chunk(rows, DI), by_chunk(rows, DI), fixed(8, DI), fixed(N, DI)],
        shapes(((T, DI), bf16), ((T, DI), bf16), ((T, DI), bf16), ((8, DI), f32), ((N, DI), f32)),
    )(gno, kept["y"], proj, w["gains"], cum, match, bc, kept["pref"], expand)
    dy = move([out_sums] + beside[1:], dy)
    dsn = relay(kept["thru"], ds_local, -1)
    dxi, dbc, dcum = call(
        intra_back_kernel,
        nc,
        [by_chunk(rows, DI), by_chunk(rows, DI), by_chunk(rows, 2 * N), by_chunk(rows, H),
         by_lead(H, rows), by_chunk(rows, 8), by_lead(1, rows), fixed(*reduce.shape)],
        [by_chunk(rows, DI), by_chunk(rows, 2 * N), by_chunk(rows, H)],
        shapes(((T, DI), f32), ((T, 2 * N), f32), ((T, H), f32)),
        [pltpu.VMEM((LANES, rows), f32)],
    )(dy, xt, bc, cum, kept["cumt"], match, segt, reduce)
    dxi = move(beside, dxi)
    rc = partial(by_chunk, rows, steps=nc)
    gp, convg, headg, rim_grad = call(
        sweep_kernel,
        nc,
        [rc(DI), rc(2 * N), rc(H), rc(DI), rc(DI), rc(DI), rc(DI), rc(2 * N), rc(H), rc(8),
         by_lead(N, DI, nc), rc(PWL),
         pl.BlockSpec((8, PWL), lambda i: (jnp.maximum((nc - 1 - i) * (rows // 8) - 1, 0), 0)),
         fixed(8, XC), fixed(8, XC), fixed(8, H), fixed(8, DI), fixed(*expand.shape),
         fixed(*reduce.shape), fixed(N, DI)],
        [rc(PWL), fixed(8, XC), fixed(8, H), fixed(8, XC)],
        shapes(((T, PWL), bf16), ((8, XC), f32), ((8, H), f32), ((8, XC), f32)),
        [pltpu.VMEM((N, DI), f32), pltpu.VMEM((rows + 8, XC), f32),
         pltpu.VMEM((rows + 16, XC), f32), pltpu.VMEM((24, XC), f32),
         pltpu.VMEM((rows, XC), f32)],
    )(dxi, dbc, dcum, dy, edy, dz, xt, bc, cum, match, kept["sin"], proj, proj, kept["rim"],
      w["convp"], w["headp"], w["gains"], expand, reduce, dsn)
    gp = move([out_sums] + beside, gp)
    returned = shifted(rim_grad, "seq", -1)
    tail = (gp[-16:, DI : DI + XC].astype(f32)
            + jnp.concatenate([jnp.zeros_like(returned), returned], 0)).astype(bf16)
    gp = lax.dynamic_update_slice(gp, tail, (T - 16, DI))
    half = PWL // 2
    in_sums, gp = fold([kept["normed"]] * 2, lambda g: [g[:, :half], g[:, half:]], gp)
    if beside:
        gp = move([in_sums, out_sums] + beside, gp)
    grad_normed = dot(gp, w["win"], ROWS)
    _, norm_pull = jax.vjp(rms_scale, kept["source"], w["norm_gain"])
    grad_source, grad_norm_gain = norm_pull(grad_normed)
    return grad_source, [in_sums, out_sums], (grad_norm_gain, convg, og[0], headg)


def bit_of(axis, bit):
    return (lax.axis_index(axis) // bit) % 2 == 1


def swap(value, axis, bit):
    return lax.ppermute(value, axis, [(i, i ^ bit) for i in range(lax.axis_size(axis))])


def bits(axis):
    count = lax.axis_size(axis)
    return [(axis, 1 << k) for k in reversed(range(count.bit_length() - 1))]


class Chains:
    def __init__(self, keeps, received):
        x = [("section", 1)]
        dp_bits = bits("dp")
        low, mid, rest = dp_bits[-1:], dp_bits[-2:-1], dp_bits[:-2]
        more = rest + bits("seq")[1:]
        orders = [mid + x + low + more, low + mid + x + more]
        self.orders = orders if len(keeps) == 2 else [low + x + mid + more]
        self.dims = [bits("seq")[1:] + dp_bits for _ in keeps]
        self.flying = list(zip(keeps, received))

    def parts(self):
        keeps, sends, steps = [], [], []
        for k, value in enumerate(self.values):
            step = self.orders[k].pop(0)
            mine = bit_of(*step)
            if step[0] == "section":
                half = value.shape[-1] // 2
                one, two = value[..., :half], value[..., half:]
                keep, send = jnp.where(mine, two, one), jnp.where(mine, one, two)
            else:
                dims = self.dims[k]
                d = dims.index(step)
                dims.remove(step)
                rows = value.shape[-2] >> (len(dims) + 1)
                grid = value.reshape((2,) * (len(dims) + 1) + (rows, value.shape[-1]))
                own = mine.astype(jnp.int32)
                keep = lax.dynamic_index_in_dim(grid, own, d, keepdims=False)
                send = lax.dynamic_index_in_dim(grid, 1 - own, d, keepdims=False)
                keep, send = (v.reshape(-1, v.shape[-1]) for v in (keep, send))
            keeps.append(keep)
            sends.append(send.astype(bf16))
            steps.append(step)
        return keeps, sends, steps

    def left(self):
        return bool(self.orders[0])


class Whole:
    def __init__(self, value):
        self.flying = []
        self.values = [value]
        self.order = bits("seq") + bits("dp")[::-1] + bits("section")

    def parts(self):
        return self.values, self.values, [self.order.pop(0)]

    def left(self):
        return bool(self.order)


def fold(lefts, rights, anchor):
    top = bits("seq")[0]
    mine = bit_of(*top)
    halves = [(v[:, : v.shape[1] // 2], v[:, v.shape[1] // 2 :]) for v in lefts]
    sends = [
        dot(jnp.where(mine, low, high), r, COLS).astype(bf16)
        for (low, high), r in zip(halves, rights(anchor))
    ]
    anchor, sends = lax.optimization_barrier((anchor, sends))
    received = [swap(v, *top) for v in sends]
    keeps = [
        dot(jnp.where(mine, high, low), r, COLS) for (low, high), r in zip(halves, rights(anchor))
    ]
    return Chains(keeps, received), anchor


def launch(chains, anchor):
    parts = [c.parts() for c in chains]
    anchor, sends = lax.optimization_barrier((anchor, [p[1] for p in parts]))
    for c, (keeps, _, steps), out in zip(chains, parts, sends):
        c.flying = [(k, swap(s, *step)) for k, s, step in zip(keeps, out, steps)]
    return anchor


def land(chains, anchor):
    received = [[r for _, r in c.flying] for c in chains]
    anchor, received = lax.optimization_barrier((anchor, received))
    for c, got in zip(chains, received):
        c.values = [k + r.astype(f32) for (k, _), r in zip(c.flying, got)]
        c.flying = []
    return anchor


def move(chains, anchor):
    chains = [c for c in chains if c.flying]
    if not chains:
        return anchor
    anchor = land(chains, anchor)
    chains = [c for c in chains if c.left()]
    return launch(chains, anchor) if chains else anchor


def seg_tables(segments, rows, heads):
    T = segments.shape[0]
    seg = segments.astype(f32)
    rim = shifted(seg[-3:], "seq", 1)
    padded = jnp.concatenate([rim, seg])
    cols = [(padded[k : k + T] == seg).astype(f32) for k in range(3)]
    chunked = seg.reshape(-1, rows)
    ends = chunked[:, -1]
    starts = jnp.concatenate([rim[-1:], ends[:-1]])
    cols.append(seg)
    cols.append((chunked == starts[:, None]).astype(f32).reshape(-1))
    cols.append((chunked == ends[:, None]).astype(f32).reshape(-1))
    match = jnp.stack(cols + [jnp.zeros_like(seg)] * 2, 1)
    head_of = jnp.arange(DI) // (DI // heads)
    one = (jnp.arange(heads)[:, None] == head_of[None, :]).astype(bf16)
    return dict(
        match=match, segt=chunked[:, None, :], rows=rows,
        expand=jnp.concatenate([one, one, one], 0), reduce=one.T,
    )


def shards(
    tokens, cotangent, segments, norm_gain, in_weight, conv_weight, conv_bias, dt_bias, decay_log,
    skip_gain, out_gain, out_weight,
):
    section = lax.axis_index("section")
    is_first = section == 0
    D = tokens.shape[-1]
    H = dt_bias.shape[-1]
    T = tokens.shape[2]
    rows = min(LANES, T)
    cut = conv_weight.shape[-1]
    everyone = ("section", "seq", "dp")
    mine = partial(lax.dynamic_index_in_dim, index=section, axis=0, keepdims=False)
    source = mine(tokens)[0]
    grad_low = mine(cotangent)[0]
    seg = seg_tables(mine(segments)[0], rows, H)

    small = jnp.concatenate(
        [norm_gain[0], conv_weight[0].reshape(-1), conv_bias[0], out_gain[0]]
    )[None]
    small = lax.all_gather(small, everyone, axis=0, tiled=True)
    small = small.reshape(2, -1, small.shape[-1]).astype(f32)
    heads_own = jnp.concatenate([dt_bias, -jnp.exp(decay_log), skip_gain], 0)
    heads_other = lax.ppermute(heads_own, "section", [(0, 1), (1, 0)])
    width = -(-in_weight.shape[2] // (4 * LANES)) * 4 * LANES
    padded = jnp.pad(in_weight, ((0, 0), (0, 0), (0, width - in_weight.shape[2])))
    win = lax.all_gather(padded, everyone, axis=1, tiled=True).reshape(2, D, -1)
    wout = lax.all_gather(out_weight, everyone, axis=1, tiled=True).reshape(2, DI, D)
    weights = []
    nd, no = norm_gain.shape[-1], out_gain.shape[-1]
    for s in range(2):
        vec = small[s]
        heads = jnp.where(section == s, heads_own, heads_other)
        taps = vec[:, nd : nd + 4 * cut].reshape(-1, 4, cut)
        taps = jnp.swapaxes(taps, 0, 1).reshape(4, -1)
        bias = vec[:, nd + 4 * cut : nd + 5 * cut].reshape(1, -1)
        gain = vec[:, nd + 5 * cut :].reshape(1, -1)
        skip = jnp.repeat(heads[2], DI // H)[None]
        weights.append(dict(
            norm_gain=vec[:, :nd].reshape(-1),
            convp=jnp.concatenate([taps, bias, jnp.zeros((3, XC), f32)], 0),
            headp=jnp.concatenate([heads, jnp.zeros((5, H), f32)], 0),
            gains=jnp.concatenate([gain, skip, jnp.zeros((6, DI), f32)], 0),
            win=win[s], wout=wout[s],
        ))

    out0, kept0 = layer_forward(source.astype(f32), weights[0], seg)
    passed = out0.astype(bf16)
    out1, kept1 = layer_forward(passed.astype(f32), weights[1], seg)
    final = out1.astype(bf16)
    got_out = swap(jnp.where(is_first, final, passed), "section", 1)

    grad1, beside, terms1 = layer_backward(grad_low, weights[1], seg, kept1, [])
    middle = (grad_low.astype(f32) + grad1).astype(bf16)
    middle, got_out = lax.optimization_barrier((middle, got_out))
    got_middle = lax.ppermute(middle, "section", [(0, 1)])
    grad0, sums, terms0 = layer_backward(middle, weights[0], seg, kept0, beside)
    first = middle.astype(f32) + grad0
    got_first = lax.ppermute(first.astype(bf16), "section", [(1, 0)])

    def both(position):
        return jnp.stack([terms0[position], terms1[position]])

    convg = both(1)
    packed = jnp.concatenate(
        [both(0).reshape(2, -1, nd),
         jnp.swapaxes(convg[:, :4].reshape(2, 4, -1, cut), 1, 2).reshape(2, -1, 4 * cut),
         convg[:, 4].reshape(2, -1, cut), both(2).reshape(2, -1, no)], -1
    )
    spare = packed.shape[-1] - 3 * H
    head_sums = jnp.pad(both(3)[:, :3].reshape(2, 1, -1), ((0, 0), (0, 0), (0, spare)))
    small = Whole(jnp.concatenate([packed, head_sums], 1))

    def join(zero, one):
        own, other = jnp.where(is_first, zero, one), jnp.where(is_first, one, zero)
        other = swap(other.astype(bf16), "section", 1).astype(f32)
        return [jnp.where(is_first, own, other), jnp.where(is_first, other, own)]

    launch([small], ())
    land([small], ())
    in1, out1 = beside
    in0, out0 = sums
    grad_out = None
    running = [in0, out0, in1, out1, small]
    while running:
        got_first = move(running, got_first)
        running = [c for c in running if c.flying or c.left()]
        waiting = [c for c in running if not c.flying]
        if waiting:
            launch(waiting, ())
        if grad_out is None and out0 not in running and out1 not in running:
            grad_out = join(out0.values[0], out1.values[0])
    section_outputs = jnp.stack(
        [jnp.where(is_first, passed, got_out), jnp.where(is_first, got_out, final)]
    )
    input_grads = jnp.stack(
        [jnp.where(is_first, first, got_middle.astype(f32)),
         jnp.where(is_first, got_first, middle).astype(f32)]
    )
    packed = jnp.where(is_first, small.values[0][0], small.values[0][1])
    head_sums = packed[-1, : 3 * H].reshape(3, H)
    place = lax.axis_index("seq") * lax.axis_size("dp") + lax.axis_index("dp")
    vec = lax.dynamic_index_in_dim(packed, place, 0, keepdims=False)
    grad_in = join(in0.values[0], in1.values[0]) + join(in0.values[1], in1.values[1])
    grad_in = jnp.concatenate(grad_in, -1)[None, :, : in_weight.shape[2]]
    grad_out = jnp.concatenate(grad_out, -1)[None]
    return (
        section_outputs[None, :, None],
        input_grads[None, :, None],
        vec[None, :nd],
        grad_in,
        vec[nd : nd + 4 * cut].reshape(1, 4, cut),
        vec[None, nd + 4 * cut : nd + 5 * cut],
        head_sums[0:1],
        head_sums[1:2],
        head_sums[2:3],
        vec[None, nd + 5 * cut :],
        grad_out,
    )


def solution(mesh):
    placed = (
        P(None, "dp", "seq", None),
        P(None, "dp", "seq", None),
        P(None, "dp", "seq"),
        P("section", ("seq", "dp")),
        P("section", ("seq", "dp"), None),
        P("section", None, ("seq", "dp")),
        P("section", ("seq", "dp")),
        P("section", None),
        P("section", None),
        P("section", None),
        P("section", ("seq", "dp")),
        P("section", ("seq", "dp"), None),
    )
    return jax.shard_map(
        shards,
        mesh=mesh,
        in_specs=placed,
        out_specs=(
            P("section", None, "dp", "seq", None),
            P("section", None, "dp", "seq", None),
            P("section", ("seq", "dp")),
            P("section", ("seq", "dp"), None),
            P("section", None, ("seq", "dp")),
            P("section", ("seq", "dp")),
            P("section", None),
            P("section", None),
            P("section", None),
            P("section", ("seq", "dp")),
            P("section", ("seq", "dp"), None),
        ),
        check_vma=False,
    )
```

```python
from functools import partial

import jax
import jax.numpy as jnp
from jax import lax
from jax.experimental import pallas as pl
from jax.experimental.pallas import tpu as pltpu
from jax.sharding import PartitionSpec as P

DI = 1536
N = 128
XC = 1792
EPS = 1e-05
MASKED = -1e30
VMEM_LIMIT = 16 * 1024 * 1024
LANES = 128

f32 = jnp.float32
bf16 = jnp.bfloat16
highest = lax.Precision.HIGHEST


def dot(a, b, contract=((1,), (0,)), precision=None):
    return lax.dot_general(
        a, b, (contract, ((), ())), precision=precision, preferred_element_type=f32
    )


ROWS = ((1,), (1,))
COLS = ((0,), (0,))


def split3(v):
    hi = v.astype(bf16)
    rest = v - hi.astype(f32)
    mid = rest.astype(bf16)
    return hi, mid, (rest - mid.astype(f32)).astype(bf16)


def widen(v, expand):
    return dot(jnp.concatenate(split3(v), 1), expand)


def narrow(v, reduce):
    return dot(v.astype(bf16), reduce)


def narrow_exact(v, reduce):
    hi, mid, lo = split3(v)
    return dot(hi, reduce) + dot(mid, reduce) + dot(lo, reduce)


def sigmoid(v):
    return 1.0 / (1.0 + jnp.exp(-v))


def softplus(v):
    return jnp.maximum(v, 0.0) + jnp.log1p(jnp.exp(-jnp.abs(v)))


def conv_forward(pad, match, convp, rows):
    out = convp[4:5, :] + convp[3:4, :] * pad[8 : 8 + rows, :]
    for k in range(3):
        out = out + convp[k : k + 1, :] * pad[5 + k : 5 + k + rows, :] * match[:, k : k + 1]
    return out


def half_masks(rows):
    lane = lax.broadcasted_iota(jnp.int32, (rows, LANES), 1)
    low = jnp.where(lane < LANES // 2, 1.0, 0.0)
    return low.astype(bf16), (1.0 - low).astype(bf16)


def prep_kernel(
    proj, rim, match, convp, headp, expand, xt_o, xs_o, bc_o, cum_o, cumt_o, sin_o, end_o, pref_o,
    thru_o, pad, state, pref,
):
    c = pl.program_id(0)
    rows = proj.shape[0]
    heads = headp.shape[1]

    @pl.when(c == 0)
    def _():
        pad[0:8, :] = rim[...]
        state[...] = jnp.zeros_like(state)
        pref[...] = jnp.ones_like(pref)

    @pl.when(c > 0)
    def _():
        pad[0:8, :] = pad[rows : rows + 8, :]

    pad[8 : 8 + rows, :] = proj[:, DI : DI + XC]
    m = match[...]
    conv = conv_forward(pad, m, convp, rows)
    act = conv * sigmoid(conv)
    dt = softplus(proj[:, DI + XC : DI + XC + heads] + headp[0:1, :])
    log_decay = dt * headp[1:2, :]
    row = lax.broadcasted_iota(jnp.int32, (rows, rows), 0)
    col = lax.broadcasted_iota(jnp.int32, (rows, rows), 1)
    lower = jnp.where(row >= col, 1.0, 0.0)
    cum = dot(lower, log_decay, precision=highest)
    cum_o[...] = cum
    cumt_o[0] = dot(
        log_decay, jnp.where(row <= col, 1.0, 0.0), COLS, precision=highest
    )
    last = cum[rows - 1 : rows, :]
    wide = widen(
        jnp.concatenate(
            [dt, jnp.exp(last - cum) * m[:, 5:6],
             jnp.broadcast_to(jnp.exp(last) * m[rows - 1 : rows, 4:5], (8, heads))], 0
        ),
        expand[...],
    )
    x = act[:, :DI]
    xt = x * wide[:rows]
    b = act[:, DI : DI + N].astype(bf16)
    xt_o[...] = xt.astype(bf16)
    xs_o[...] = x.astype(bf16)
    bc_o[...] = act[:, DI:].astype(bf16)
    sin_o[0] = state[...].astype(bf16)
    pref_o[0] = pref[...]
    through = wide[2 * rows :]
    state[...] = through[0:1] * state[...] + dot(
        b, (xt * wide[rows : 2 * rows]).astype(bf16), COLS
    )
    pref[...] = pref[...] * through
    end_o[...] = state[...]
    thru_o[...] = pref[...]


def decay_mask(seg_col, seg_row, transposed):
    rows = seg_col.shape[0]
    row = lax.broadcasted_iota(jnp.int32, (rows, rows), 0)
    col = lax.broadcasted_iota(jnp.int32, (rows, rows), 1)
    order = (col >= row) if transposed else (row >= col)
    return (seg_col == seg_row) & order


def intra_kernel(xt, bc, cum, cumt, match, segt, yi_o):
    rows = xt.shape[0]
    mask = decay_mask(match[:, 3:4], segt[0], False)
    scores = dot(bc[:, N:], bc[:, :N], ROWS)
    low, high = half_masks(rows)
    for p in range(xt.shape[1] // LANES):
        mixes = []
        for h in (2 * p, 2 * p + 1):
            gap = cum[:, h : h + 1] - cumt[0, h : h + 1, :]
            mixes.append((jnp.exp(jnp.where(mask, gap, MASKED)) * scores).astype(bf16))
        xp = xt[:, LANES * p : LANES * (p + 1)]
        blocks = jnp.concatenate([xp * low, xp * high], 0)
        yi_o[:, LANES * p : LANES * (p + 1)] = dot(jnp.concatenate(mixes, 1), blocks)


def finish_kernel(
    yi, xs, bc, cum, match, sin_l, pref, dev, z_ref, gains, expand, y_o, no_o, sin_o
):
    sin = (sin_l[0].astype(f32) + pref[0, 0:1, :] * dev[...]).astype(bf16)
    sin_o[0] = sin
    carry = widen(jnp.exp(cum[...]) * match[:, 4:5], expand[...])
    y = yi[...] + carry * dot(bc[:, N:], sin) + gains[1:2, :] * xs[...].astype(f32)
    y_o[...] = y
    z = z_ref[...]
    g = y * z * sigmoid(z)
    r = lax.rsqrt(jnp.mean(g * g, -1, keepdims=True) + EPS)
    no_o[...] = (g * r * gains[0:1, :]).astype(bf16)


def gate_back_kernel(
    gno, y_ref, z_ref, gains, cum, match, bc, pref, expand, dy_o, dz_o, edy_o, og_o, ds_o
):
    @pl.when(pl.program_id(0) == 0)
    def _():
        og_o[...] = jnp.zeros_like(og_o)
        ds_o[...] = jnp.zeros_like(ds_o)

    z = z_ref[...]
    y = y_ref[...]
    sz = sigmoid(z)
    silu = z * sz
    g = y * silu
    r = lax.rsqrt(jnp.mean(g * g, -1, keepdims=True) + EPS)
    gr = g * r
    gv = gno[...]
    og_o[...] += jnp.broadcast_to(jnp.sum(gv * gr, 0, keepdims=True), og_o.shape)
    gn = gv * gains[0:1, :]
    dg = r * (gn - gr * jnp.mean(gn * gr, -1, keepdims=True))
    dy = dg * silu
    dy_o[...] = dy.astype(bf16)
    dz_o[...] = (dg * y * sz * (1.0 + z * (1.0 - sz))).astype(bf16)
    edy = (widen(jnp.exp(cum[...]) * match[:, 4:5], expand[...]) * dy).astype(bf16)
    edy_o[...] = edy
    ds_o[...] += pref[0, 0:1, :] * dot(bc[:, N:], edy, COLS)


def intra_back_kernel(
    dy, xt, bc, cum, cumt, match, segt, reduce, dxi_o, dbc_o, dcum_o, rs
):
    rows = xt.shape[0]
    mask = decay_mask(match[:, 3:4], segt[0], True)
    b = bc[:, :N]
    c = bc[:, N:]
    scores = dot(b, c, ROWS)
    low, high = half_masks(rows)
    rs[...] = jnp.zeros_like(rs)
    dscores = jnp.zeros((rows, rows), f32)
    for p in range(xt.shape[1] // LANES):
        xp = xt[:, LANES * p : LANES * (p + 1)]
        dyp = dy[:, LANES * p : LANES * (p + 1)]
        dmix = dot(jnp.concatenate([xp * low, xp * high], 0), dyp, ROWS)
        mixes = []
        for j in range(2):
            h = 2 * p + j
            gap = cumt[0, h : h + 1, :] - cum[:, h : h + 1]
            decay = jnp.exp(jnp.where(mask, gap, MASKED))
            dm = dmix[rows * j : rows * (j + 1)]
            dscores = dscores + dm * decay
            mix = (decay * scores).astype(bf16)
            mixes.append(mix)
            rs[h : h + 1, :] = jnp.sum(dm * mix.astype(f32), 0, keepdims=True)
        blocks = jnp.concatenate([dyp * low, dyp * high], 0)
        dxi_o[:, LANES * p : LANES * (p + 1)] = dot(jnp.concatenate(mixes, 1), blocks)
    ds = dscores.astype(bf16)
    dbc_o[:, :N] = dot(ds, c)
    dbc_o[:, N:] = dot(ds, b, COLS)
    heads = cum.shape[1]
    cols = narrow_exact(xt[...].astype(f32) * dxi_o[...], reduce[...])
    dcum_o[...] = jnp.transpose(rs[...])[:, :heads] - cols


def sweep_kernel(
    dxi, dbc, dcum, dy, edy, dz, xt, bc, cum, match, sin_ref, proj, before, rim, convp, headp,
    gains, expand, reduce, dsn, gp_o, convg_o, headg_o, rim_o, ds, pad, buf, carry, acc,
):
    i = pl.program_id(0)
    steps = pl.num_programs(0)
    rows = xt.shape[0]
    heads = cum.shape[1]

    @pl.when(i == 0)
    def _():
        ds[...] = dsn[...]
        carry[...] = jnp.zeros_like(carry)
        convg_o[...] = jnp.zeros_like(convg_o)
        headg_o[...] = jnp.zeros_like(headg_o)

    @pl.when(i == steps - 1)
    def _():
        pad[0:8, :] = rim[...]

    @pl.when(i < steps - 1)
    def _():
        pad[0:8, :] = before[:, DI : DI + XC]

    pad[8 : 8 + rows, :] = proj[:, DI : DI + XC]
    m = match[...]
    conv = conv_forward(pad, m, convp, rows)
    sc = sigmoid(conv)
    act = conv * sc
    x = act[:, :DI]
    raw = proj[:, DI + XC : DI + XC + heads] + headp[0:1, :]
    dt = softplus(raw)
    rate = headp[1:2, :]
    cumv = cum[...]
    last = cumv[rows - 1 : rows, :]
    thru = jnp.exp(last) * m[rows - 1 : rows, 4:5]
    wide = widen(
        jnp.concatenate(
            [dt, jnp.exp(last - cumv) * m[:, 5:6], jnp.broadcast_to(thru, (8, heads))], 0
        ),
        expand[...],
    )
    dt_e = wide[:rows]
    tail_e = wide[rows : 2 * rows]
    thru_e = wide[2 * rows : 2 * rows + 1]
    b = bc[:, :N]
    c = bc[:, N:]
    state_grad = ds[...]
    low_grad = state_grad.astype(bf16)
    sin = sin_ref[0]
    xtv = xt[...].astype(f32)
    dyv = dy[...].astype(f32)
    edyb = edy[...]
    dx_in = tail_e * dot(b, low_grad)
    dxt = dxi[...] + dx_in
    stacked = jnp.concatenate(
        [
            (xtv * dx_in).astype(bf16),
            (edyb.astype(f32) * dot(c, sin)).astype(bf16),
            (x * dxt).astype(bf16),
            (x * dyv).astype(bf16),
        ],
        0,
    )
    sums = dot(stacked, reduce[...])
    db = dbc[:, :N] + dot((tail_e * xtv).astype(bf16), low_grad, ROWS)
    dc = dbc[:, N:] + dot(edyb, sin, ROWS)
    held = jnp.sum(state_grad * sin.astype(f32), 0, keepdims=True)
    dthru = narrow_exact(jnp.broadcast_to(held, (8, held.shape[1])), reduce[...])[0:1] * thru
    ds[...] = thru_e * state_grad + dot(c, edyb, COLS)
    row = lax.broadcasted_iota(jnp.int32, (rows, rows), 0)
    col = lax.broadcasted_iota(jnp.int32, (rows, rows), 1)
    dlog = (
        dot(jnp.where(row <= col, 1.0, 0.0), dcum[...] + sums[rows : 2 * rows], precision=highest)
        + dot(jnp.where(row > col, 1.0, 0.0), sums[:rows], precision=highest)
        + dthru
    )
    ddt = sums[2 * rows : 3 * rows] + dlog * rate
    draw = ddt * sigmoid(raw)
    headg_o[0:1, :] += jnp.sum(draw, 0, keepdims=True)
    headg_o[1:2, :] += jnp.sum(dlog * dt, 0, keepdims=True) * rate
    headg_o[2:3, :] += jnp.sum(sums[3 * rows :], 0, keepdims=True)
    gp_o[:, :DI] = dz[...]
    gp_o[:, DI + XC :] = jnp.zeros((rows, gp_o.shape[1] - DI - XC), bf16)
    gp_o[:, DI + XC : DI + XC + heads] = draw.astype(bf16)
    dact = jnp.concatenate([dt_e * dxt + gains[1:2, :] * dyv, db, dc], 1)
    dconv = dact * (sc * (1.0 + conv * (1.0 - sc)))
    convg_o[4:5, :] += jnp.sum(dconv, 0, keepdims=True)
    convg_o[3:4, :] += jnp.sum(dconv * pad[8 : 8 + rows, :], 0, keepdims=True)
    acc[...] = dconv * convp[3:4, :]
    rim_sum = jnp.zeros((8, XC), f32)
    for k in range(3):
        v = dconv * m[:, k : k + 1]
        convg_o[k : k + 1, :] += jnp.sum(v * pad[5 + k : 5 + k + rows, :], 0, keepdims=True)
        v = v * convp[k : k + 1, :]
        buf[0:8, :] = jnp.zeros((8, XC), f32)
        buf[8 : 8 + rows, :] = v
        buf[8 + rows : 16 + rows, :] = carry[8 * k : 8 * k + 8, :]
        shift = 3 - k
        acc[...] += buf[8 + shift : 8 + shift + rows, :]
        rim_sum = rim_sum + buf[shift : 8 + shift, :]
        carry[8 * k : 8 * k + 8, :] = v[0:8, :]
    gp_o[:, DI : DI + XC] = acc[...].astype(bf16)
    rim_o[...] = rim_sum


def shapes(*specs):
    return [jax.ShapeDtypeStruct(s, d) for s, d in specs]


def by_chunk(rows, cols, steps=None):
    if steps is None:
        return pl.BlockSpec((rows, cols), lambda i: (i, 0))
    return pl.BlockSpec((rows, cols), lambda i: (steps - 1 - i, 0))


def by_lead(a, b, steps=None):
    if steps is None:
        return pl.BlockSpec((1, a, b), lambda i: (i, 0, 0))
    return pl.BlockSpec((1, a, b), lambda i: (steps - 1 - i, 0, 0))


def fixed(*shape):
    return pl.BlockSpec(shape, lambda i: (0,) * len(shape))


def call(kernel, steps, ins, outs, out_shape, scratch=()):
    return pl.pallas_call(
        kernel,
        grid=(steps,),
        in_specs=ins,
        out_specs=outs,
        out_shape=out_shape,
        scratch_shapes=scratch,
        compiler_params=pltpu.CompilerParams(
            dimension_semantics=("arbitrary",), vmem_limit_bytes=VMEM_LIMIT
        ),
        cost_estimate=pl.CostEstimate(flops=1000, bytes_accessed=1000, transcendentals=0),
    )


def shifted(value, axis, steps):
    count = lax.axis_size(axis)
    initial, last = (max(0, -steps), min(count, count - steps))
    return lax.ppermute(value, axis, [(source, source + steps) for source in range(initial, last)])


def relay(through, local, steps):
    incoming = shifted(local, "seq", steps)
    for _ in range(lax.axis_size("seq") - 2):
        incoming = shifted(through[0:1] * incoming + local, "seq", steps)
    return incoming


def rms_scale(values, gain):
    return values * lax.rsqrt(jnp.mean(values * values, -1, keepdims=True) + EPS) * gain


def layer_forward(source, w, seg):
    match, segt, rows = seg["match"], seg["segt"], seg["rows"]
    T = source.shape[0]
    nc = T // rows
    H = w["headp"].shape[1]
    PWL = w["win"].shape[1]
    normed = rms_scale(source, w["norm_gain"]).astype(bf16)
    proj = dot(normed, w["win"])
    rim = shifted(proj[-8:, DI : DI + XC], "seq", 1)
    expand = seg["expand"]
    xt, xs, bc, cum, cumt, sin_l, end, pref, thru = call(
        prep_kernel,
        nc,
        [by_chunk(rows, PWL), fixed(8, XC), by_chunk(rows, 8), fixed(8, XC), fixed(8, H),
         fixed(*expand.shape)],
        [by_chunk(rows, DI), by_chunk(rows, DI), by_chunk(rows, 2 * N), by_chunk(rows, H),
         by_lead(H, rows), by_lead(N, DI), fixed(N, DI), by_lead(8, DI), fixed(8, DI)],
        shapes(((T, DI), bf16), ((T, DI), bf16), ((T, 2 * N), bf16), ((T, H), f32),
               ((nc, H, rows), f32), ((nc, N, DI), bf16), ((N, DI), f32), ((nc, 8, DI), f32),
               ((8, DI), f32)),
        [pltpu.VMEM((rows + 8, XC), f32), pltpu.VMEM((N, DI), f32), pltpu.VMEM((8, DI), f32)],
    )(proj, rim, match, w["convp"], w["headp"], expand)
    dev = relay(thru, end, 1)
    yi = call(
        intra_kernel,
        nc,
        [by_chunk(rows, DI), by_chunk(rows, 2 * N), by_chunk(rows, H), by_lead(H, rows),
         by_chunk(rows, 8), by_lead(1, rows)],
        by_chunk(rows, DI),
        jax.ShapeDtypeStruct((T, DI), f32),
    )(xt, bc, cum, cumt, match, segt)
    y, normed_out, sin = call(
        finish_kernel,
        nc,
        [by_chunk(rows, DI), by_chunk(rows, DI), by_chunk(rows, 2 * N), by_chunk(rows, H),
         by_chunk(rows, 8), by_lead(N, DI), by_lead(8, DI), fixed(N, DI), by_chunk(rows, DI),
         fixed(8, DI), fixed(*expand.shape)],
        [by_chunk(rows, DI), by_chunk(rows, DI), by_lead(N, DI)],
        shapes(((T, DI), f32), ((T, DI), bf16), ((nc, N, DI), bf16)),
    )(yi, xs, bc, cum, match, sin_l, pref, dev, proj, w["gains"], expand)
    out = source + dot(normed_out, w["wout"])
    kept = dict(
        source=source, normed=normed, proj=proj, rim=rim, xt=xt, bc=bc, cum=cum, cumt=cumt,
        pref=pref, thru=thru, y=y, normed_out=normed_out, sin=sin,
    )
    return out, kept


def layer_backward(grad_low, w, seg, kept, beside):
    match, segt, rows = seg["match"], seg["segt"], seg["rows"]
    T = grad_low.shape[0]
    nc = T // rows
    H = w["headp"].shape[1]
    PWL = w["win"].shape[1]
    expand, reduce = seg["expand"], seg["reduce"]
    proj, bc, cum, xt = kept["proj"], kept["bc"], kept["cum"], kept["xt"]
    grad_low = move(beside, grad_low)
    out_sums, grad_low = fold([kept["normed_out"]], lambda g: [g], grad_low)
    gno = dot(grad_low, w["wout"], ROWS)
    dy, dz, edy, og, ds_local = call(
        gate_back_kernel,
        nc,
        [by_chunk(rows, DI), by_chunk(rows, DI), by_chunk(rows, DI), fixed(8, DI),
         by_chunk(rows, H), by_chunk(rows, 8), by_chunk(rows, 2 * N), by_lead(8, DI),
         fixed(*expand.shape)],
        [by_chunk(rows, DI), by_chunk(rows, DI), by_chunk(rows, DI), fixed(8, DI), fixed(N, DI)],
        shapes(((T, DI), bf16), ((T, DI), bf16), ((T, DI), bf16), ((8, DI), f32), ((N, DI), f32)),
    )(gno, kept["y"], proj, w["gains"], cum, match, bc, kept["pref"], expand)
    dy = move([out_sums] + beside[1:], dy)
    dsn = relay(kept["thru"], ds_local, -1)
    dxi, dbc, dcum = call(
        intra_back_kernel,
        nc,
        [by_chunk(rows, DI), by_chunk(rows, DI), by_chunk(rows, 2 * N), by_chunk(rows, H),
         by_lead(H, rows), by_chunk(rows, 8), by_lead(1, rows), fixed(*reduce.shape)],
        [by_chunk(rows, DI), by_chunk(rows, 2 * N), by_chunk(rows, H)],
        shapes(((T, DI), f32), ((T, 2 * N), f32), ((T, H), f32)),
        [pltpu.VMEM((LANES, rows), f32)],
    )(dy, xt, bc, cum, kept["cumt"], match, segt, reduce)
    dxi = move(beside, dxi)
    rc = partial(by_chunk, rows, steps=nc)
    gp, convg, headg, rim_grad = call(
        sweep_kernel,
        nc,
        [rc(DI), rc(2 * N), rc(H), rc(DI), rc(DI), rc(DI), rc(DI), rc(2 * N), rc(H), rc(8),
         by_lead(N, DI, nc), rc(PWL),
         pl.BlockSpec((8, PWL), lambda i: (jnp.maximum((nc - 1 - i) * (rows // 8) - 1, 0), 0)),
         fixed(8, XC), fixed(8, XC), fixed(8, H), fixed(8, DI), fixed(*expand.shape),
         fixed(*reduce.shape), fixed(N, DI)],
        [rc(PWL), fixed(8, XC), fixed(8, H), fixed(8, XC)],
        shapes(((T, PWL), bf16), ((8, XC), f32), ((8, H), f32), ((8, XC), f32)),
        [pltpu.VMEM((N, DI), f32), pltpu.VMEM((rows + 8, XC), f32),
         pltpu.VMEM((rows + 16, XC), f32), pltpu.VMEM((24, XC), f32),
         pltpu.VMEM((rows, XC), f32)],
    )(dxi, dbc, dcum, dy, edy, dz, xt, bc, cum, match, kept["sin"], proj, proj, kept["rim"],
      w["convp"], w["headp"], w["gains"], expand, reduce, dsn)
    gp = move([out_sums] + beside, gp)
    returned = shifted(rim_grad, "seq", -1)
    tail = (gp[-16:, DI : DI + XC].astype(f32)
            + jnp.concatenate([jnp.zeros_like(returned), returned], 0)).astype(bf16)
    gp = lax.dynamic_update_slice(gp, tail, (T - 16, DI))
    half = PWL // 2
    in_sums, gp = fold([kept["normed"]] * 2, lambda g: [g[:, :half], g[:, half:]], gp)
    if beside:
        gp = move([in_sums, out_sums] + beside, gp)
    grad_normed = dot(gp, w["win"], ROWS)
    _, norm_pull = jax.vjp(rms_scale, kept["source"], w["norm_gain"])
    grad_source, grad_norm_gain = norm_pull(grad_normed)
    return grad_source, [in_sums, out_sums], (grad_norm_gain, convg, og[0], headg)


def bit_of(axis, bit):
    return (lax.axis_index(axis) // bit) % 2 == 1


def swap(value, axis, bit):
    return lax.ppermute(value, axis, [(i, i ^ bit) for i in range(lax.axis_size(axis))])


def bits(axis):
    count = lax.axis_size(axis)
    return [(axis, 1 << k) for k in reversed(range(count.bit_length() - 1))]


class Chains:
    def __init__(self, keeps, received):
        x = [("section", 1)]
        dp_bits = bits("dp")
        low, mid, rest = dp_bits[-1:], dp_bits[-2:-1], dp_bits[:-2]
        more = rest + bits("seq")[1:]
        orders = [mid + x + low + more, low + mid + x + more]
        self.orders = orders if len(keeps) == 2 else [low + x + mid + more]
        self.dims = [bits("seq")[1:] + dp_bits for _ in keeps]
        self.flying = list(zip(keeps, received))

    def parts(self):
        keeps, sends, steps = [], [], []
        for k, value in enumerate(self.values):
            step = self.orders[k].pop(0)
            mine = bit_of(*step)
            if step[0] == "section":
                half = value.shape[-1] // 2
                one, two = value[..., :half], value[..., half:]
                keep, send = jnp.where(mine, two, one), jnp.where(mine, one, two)
            else:
                dims = self.dims[k]
                d = dims.index(step)
                dims.remove(step)
                rows = value.shape[-2] >> (len(dims) + 1)
                grid = value.reshape((2,) * (len(dims) + 1) + (rows, value.shape[-1]))
                own = mine.astype(jnp.int32)
                keep = lax.dynamic_index_in_dim(grid, own, d, keepdims=False)
                send = lax.dynamic_index_in_dim(grid, 1 - own, d, keepdims=False)
                keep, send = (v.reshape(-1, v.shape[-1]) for v in (keep, send))
            keeps.append(keep)
            sends.append(send.astype(bf16))
            steps.append(step)
        return keeps, sends, steps

    def left(self):
        return bool(self.orders[0])


class Whole:
    def __init__(self, value):
        self.flying = []
        self.values = [value]
        self.order = bits("seq") + bits("dp")[::-1] + bits("section")

    def parts(self):
        return self.values, self.values, [self.order.pop(0)]

    def left(self):
        return bool(self.order)


def spread(values):
    section, seq, dp = bits("section"), bits("seq"), bits("dp")
    present = []
    for step in dp[:-2] + dp[-2:-1] + section + dp[-1:] + seq:
        place = sum((section + seq + dp).index(p) < (section + seq + dp).index(step) for p in present)
        present.append(step)
        mine = bit_of(*step)
        got = [swap(v, *step) for v in values]
        values = [
            jnp.stack([jnp.where(mine, g, v), jnp.where(mine, v, g)], place)
            for v, g in zip(values, got)
        ]
    return values


def fold(lefts, rights, anchor):
    top = bits("seq")[0]
    mine = bit_of(*top)
    halves = [(v[:, : v.shape[1] // 2], v[:, v.shape[1] // 2 :]) for v in lefts]
    sends = [
        dot(jnp.where(mine, low, high), r, COLS).astype(bf16)
        for (low, high), r in zip(halves, rights(anchor))
    ]
    anchor, sends = lax.optimization_barrier((anchor, sends))
    received = [swap(v, *top) for v in sends]
    keeps = [
        dot(jnp.where(mine, high, low), r, COLS) for (low, high), r in zip(halves, rights(anchor))
    ]
    return Chains(keeps, received), anchor


def launch(chains, anchor):
    parts = [c.parts() for c in chains]
    anchor, sends = lax.optimization_barrier((anchor, [p[1] for p in parts]))
    for c, (keeps, _, steps), out in zip(chains, parts, sends):
        c.flying = [(k, swap(s, *step)) for k, s, step in zip(keeps, out, steps)]
    return anchor


def land(chains, anchor):
    received = [[r for _, r in c.flying] for c in chains]
    anchor, received = lax.optimization_barrier((anchor, received))
    for c, got in zip(chains, received):
        c.values = [k + r.astype(f32) for (k, _), r in zip(c.flying, got)]
        c.flying = []
    return anchor


def move(chains, anchor):
    chains = [c for c in chains if c.flying]
    if not chains:
        return anchor
    anchor = land(chains, anchor)
    chains = [c for c in chains if c.left()]
    return launch(chains, anchor) if chains else anchor


def seg_tables(segments, rows, heads):
    T = segments.shape[0]
    seg = segments.astype(f32)
    rim = shifted(seg[-3:], "seq", 1)
    padded = jnp.concatenate([rim, seg])
    cols = [(padded[k : k + T] == seg).astype(f32) for k in range(3)]
    chunked = seg.reshape(-1, rows)
    ends = chunked[:, -1]
    starts = jnp.concatenate([rim[-1:], ends[:-1]])
    cols.append(seg)
    cols.append((chunked == starts[:, None]).astype(f32).reshape(-1))
    cols.append((chunked == ends[:, None]).astype(f32).reshape(-1))
    match = jnp.stack(cols + [jnp.zeros_like(seg)] * 2, 1)
    head_of = jnp.arange(DI) // (DI // heads)
    one = (jnp.arange(heads)[:, None] == head_of[None, :]).astype(bf16)
    return dict(
        match=match, segt=chunked[:, None, :], rows=rows,
        expand=jnp.concatenate([one, one, one], 0), reduce=one.T,
    )


def shards(
    tokens, cotangent, segments, norm_gain, in_weight, conv_weight, conv_bias, dt_bias, decay_log,
    skip_gain, out_gain, out_weight,
):
    section = lax.axis_index("section")
    is_first = section == 0
    D = tokens.shape[-1]
    H = dt_bias.shape[-1]
    T = tokens.shape[2]
    rows = min(LANES, T)
    cut = conv_weight.shape[-1]
    everyone = ("section", "seq", "dp")
    mine = partial(lax.dynamic_index_in_dim, index=section, axis=0, keepdims=False)
    source = mine(tokens)[0]
    grad_low = mine(cotangent)[0]
    seg = seg_tables(mine(segments)[0], rows, H)

    small = jnp.concatenate(
        [norm_gain[0], conv_weight[0].reshape(-1), conv_bias[0], out_gain[0]]
    )[None]
    wout, small = spread([out_weight[0], small])
    wout = wout.reshape(2, DI, D)
    small = small.reshape(2, -1, small.shape[-1]).astype(f32)
    heads_own = jnp.concatenate([dt_bias, -jnp.exp(decay_log), skip_gain], 0)
    heads_other = lax.ppermute(heads_own, "section", [(0, 1), (1, 0)])
    width = -(-in_weight.shape[2] // (4 * LANES)) * 4 * LANES
    padded = jnp.pad(in_weight, ((0, 0), (0, 0), (0, width - in_weight.shape[2])))
    win = lax.all_gather(padded, everyone, axis=1, tiled=True).reshape(2, D, -1)
    weights = []
    nd, no = norm_gain.shape[-1], out_gain.shape[-1]
    for s in range(2):
        vec = small[s]
        heads = jnp.where(section == s, heads_own, heads_other)
        taps = vec[:, nd : nd + 4 * cut].reshape(-1, 4, cut)
        taps = jnp.swapaxes(taps, 0, 1).reshape(4, -1)
        bias = vec[:, nd + 4 * cut : nd + 5 * cut].reshape(1, -1)
        gain = vec[:, nd + 5 * cut :].reshape(1, -1)
        skip = jnp.repeat(heads[2], DI // H)[None]
        weights.append(dict(
            norm_gain=vec[:, :nd].reshape(-1),
            convp=jnp.concatenate([taps, bias, jnp.zeros((3, XC), f32)], 0),
            headp=jnp.concatenate([heads, jnp.zeros((5, H), f32)], 0),
            gains=jnp.concatenate([gain, skip, jnp.zeros((6, DI), f32)], 0),
            win=win[s], wout=wout[s],
        ))

    out0, kept0 = layer_forward(source.astype(f32), weights[0], seg)
    passed = out0.astype(bf16)
    out1, kept1 = layer_forward(passed.astype(f32), weights[1], seg)
    final = out1.astype(bf16)
    got_out = swap(jnp.where(is_first, final, passed), "section", 1)

    grad1, beside, terms1 = layer_backward(grad_low, weights[1], seg, kept1, [])
    middle = (grad_low.astype(f32) + grad1).astype(bf16)
    middle, got_out = lax.optimization_barrier((middle, got_out))
    got_middle = lax.ppermute(middle, "section", [(0, 1)])
    grad0, sums, terms0 = layer_backward(middle, weights[0], seg, kept0, beside)
    first = middle.astype(f32) + grad0
    got_first = lax.ppermute(first.astype(bf16), "section", [(1, 0)])

    def both(position):
        return jnp.stack([terms0[position], terms1[position]])

    convg = both(1)
    packed = jnp.concatenate(
        [both(0).reshape(2, -1, nd),
         jnp.swapaxes(convg[:, :4].reshape(2, 4, -1, cut), 1, 2).reshape(2, -1, 4 * cut),
         convg[:, 4].reshape(2, -1, cut), both(2).reshape(2, -1, no)], -1
    )
    spare = packed.shape[-1] - 3 * H
    head_sums = jnp.pad(both(3)[:, :3].reshape(2, 1, -1), ((0, 0), (0, 0), (0, spare)))
    small = Whole(jnp.concatenate([packed, head_sums], 1))

    def join(zero, one):
        own, other = jnp.where(is_first, zero, one), jnp.where(is_first, one, zero)
        other = swap(other.astype(bf16), "section", 1).astype(f32)
        return [jnp.where(is_first, own, other), jnp.where(is_first, other, own)]

    launch([small], ())
    land([small], ())
    in1, out1 = beside
    in0, out0 = sums
    grad_out = None
    running = [in0, out0, in1, out1, small]
    while running:
        got_first = move(running, got_first)
        running = [c for c in running if c.flying or c.left()]
        waiting = [c for c in running if not c.flying]
        if waiting:
            launch(waiting, ())
        if grad_out is None and out0 not in running and out1 not in running:
            grad_out = join(out0.values[0], out1.values[0])
    section_outputs = jnp.stack(
        [jnp.where(is_first, passed, got_out), jnp.where(is_first, got_out, final)]
    )
    input_grads = jnp.stack(
        [jnp.where(is_first, first, got_middle.astype(f32)),
         jnp.where(is_first, got_first, middle).astype(f32)]
    )
    packed = jnp.where(is_first, small.values[0][0], small.values[0][1])
    head_sums = packed[-1, : 3 * H].reshape(3, H)
    place = lax.axis_index("seq") * lax.axis_size("dp") + lax.axis_index("dp")
    vec = lax.dynamic_index_in_dim(packed, place, 0, keepdims=False)
    grad_in = join(in0.values[0], in1.values[0]) + join(in0.values[1], in1.values[1])
    grad_in = jnp.concatenate(grad_in, -1)[None, :, : in_weight.shape[2]]
    grad_out = jnp.concatenate(grad_out, -1)[None]
    return (
        section_outputs[None, :, None],
        input_grads[None, :, None],
        vec[None, :nd],
        grad_in,
        vec[nd : nd + 4 * cut].reshape(1, 4, cut),
        vec[None, nd + 4 * cut : nd + 5 * cut],
        head_sums[0:1],
        head_sums[1:2],
        head_sums[2:3],
        vec[None, nd + 5 * cut :],
        grad_out,
    )


def solution(mesh):
    placed = (
        P(None, "dp", "seq", None),
        P(None, "dp", "seq", None),
        P(None, "dp", "seq"),
        P("section", ("seq", "dp")),
        P("section", ("seq", "dp"), None),
        P("section", None, ("seq", "dp")),
        P("section", ("seq", "dp")),
        P("section", None),
        P("section", None),
        P("section", None),
        P("section", ("seq", "dp")),
        P("section", ("seq", "dp"), None),
    )
    return jax.shard_map(
        shards,
        mesh=mesh,
        in_specs=placed,
        out_specs=(
            P("section", None, "dp", "seq", None),
            P("section", None, "dp", "seq", None),
            P("section", ("seq", "dp")),
            P("section", ("seq", "dp"), None),
            P("section", None, ("seq", "dp")),
            P("section", ("seq", "dp")),
            P("section", None),
            P("section", None),
            P("section", None),
            P("section", ("seq", "dp")),
            P("section", ("seq", "dp"), None),
        ),
        check_vma=False,
    )
```

```python
from functools import partial

import jax
import jax.numpy as jnp
from jax import lax
from jax.experimental import pallas as pl
from jax.experimental.pallas import tpu as pltpu
from jax.sharding import PartitionSpec as P

DI = 1536
N = 128
XC = 1792
EPS = 1e-05
MASKED = -1e30
VMEM_LIMIT = 16 * 1024 * 1024
LANES = 128

f32 = jnp.float32
bf16 = jnp.bfloat16
highest = lax.Precision.HIGHEST


def dot(a, b, contract=((1,), (0,)), precision=None):
    return lax.dot_general(
        a, b, (contract, ((), ())), precision=precision, preferred_element_type=f32
    )


ROWS = ((1,), (1,))
COLS = ((0,), (0,))


def split3(v):
    hi = v.astype(bf16)
    rest = v - hi.astype(f32)
    mid = rest.astype(bf16)
    return hi, mid, (rest - mid.astype(f32)).astype(bf16)


def widen(v, expand):
    return dot(jnp.concatenate(split3(v), 1), expand)


def narrow(v, reduce):
    return dot(v.astype(bf16), reduce)


def narrow_exact(v, reduce):
    hi, mid, lo = split3(v)
    return dot(hi, reduce) + dot(mid, reduce) + dot(lo, reduce)


def sigmoid(v):
    return 0.5 * jnp.tanh(0.5 * v) + 0.5


def softplus(v):
    return jnp.maximum(v, 0.0) + jnp.log1p(jnp.exp(-jnp.abs(v)))


def conv_forward(pad, match, convp, rows):
    out = convp[4:5, :] + convp[3:4, :] * pad[8 : 8 + rows, :]
    for k in range(3):
        out = out + convp[k : k + 1, :] * pad[5 + k : 5 + k + rows, :] * match[:, k : k + 1]
    return out


def half_masks(rows):
    lane = lax.broadcasted_iota(jnp.int32, (rows, LANES), 1)
    low = jnp.where(lane < LANES // 2, 1.0, 0.0)
    return low.astype(bf16), (1.0 - low).astype(bf16)


def prep_kernel(
    proj, rim, match, convp, headp, expand, xt_o, xs_o, bc_o, cum_o, cumt_o, sin_o, end_o, pref_o,
    thru_o, pad, state, pref,
):
    c = pl.program_id(0)
    rows = proj.shape[0]
    heads = headp.shape[1]

    @pl.when(c == 0)
    def _():
        pad[0:8, :] = rim[...]
        state[...] = jnp.zeros_like(state)
        pref[...] = jnp.ones_like(pref)

    @pl.when(c > 0)
    def _():
        pad[0:8, :] = pad[rows : rows + 8, :]

    pad[8 : 8 + rows, :] = proj[:, DI : DI + XC]
    m = match[...]
    conv = conv_forward(pad, m, convp, rows)
    act = conv * sigmoid(conv)
    dt = softplus(proj[:, DI + XC : DI + XC + heads] + headp[0:1, :])
    log_decay = dt * headp[1:2, :]
    row = lax.broadcasted_iota(jnp.int32, (rows, rows), 0)
    col = lax.broadcasted_iota(jnp.int32, (rows, rows), 1)
    lower = jnp.where(row >= col, 1.0, 0.0)
    cum = dot(lower, log_decay, precision=highest)
    cum_o[...] = cum
    cumt_o[0] = dot(
        log_decay, jnp.where(row <= col, 1.0, 0.0), COLS, precision=highest
    )
    last = cum[rows - 1 : rows, :]
    wide = widen(
        jnp.concatenate(
            [dt, jnp.exp(last - cum) * m[:, 5:6],
             jnp.broadcast_to(jnp.exp(last) * m[rows - 1 : rows, 4:5], (8, heads))], 0
        ),
        expand[...],
    )
    x = act[:, :DI]
    xt = x * wide[:rows]
    b = act[:, DI : DI + N].astype(bf16)
    xt_o[...] = xt.astype(bf16)
    xs_o[...] = x.astype(bf16)
    bc_o[...] = act[:, DI:].astype(bf16)
    sin_o[0] = state[...].astype(bf16)
    pref_o[0] = pref[...]
    through = wide[2 * rows :]
    state[...] = through[0:1] * state[...] + dot(
        b, (xt * wide[rows : 2 * rows]).astype(bf16), COLS
    )
    pref[...] = pref[...] * through
    end_o[...] = state[...]
    thru_o[...] = pref[...]


def decay_mask(seg_col, seg_row, transposed):
    rows = seg_col.shape[0]
    row = lax.broadcasted_iota(jnp.int32, (rows, rows), 0)
    col = lax.broadcasted_iota(jnp.int32, (rows, rows), 1)
    order = (col >= row) if transposed else (row >= col)
    return (seg_col == seg_row) & order


def intra_kernel(xt, bc, cum, cumt, match, segt, yi_o):
    rows = xt.shape[0]
    mask = decay_mask(match[:, 3:4], segt[0], False)
    scores = dot(bc[:, N:], bc[:, :N], ROWS)
    low, high = half_masks(rows)
    for p in range(xt.shape[1] // LANES):
        mixes = []
        for h in (2 * p, 2 * p + 1):
            gap = cum[:, h : h + 1] - cumt[0, h : h + 1, :]
            mixes.append((jnp.exp(jnp.where(mask, gap, MASKED)) * scores).astype(bf16))
        xp = xt[:, LANES * p : LANES * (p + 1)]
        blocks = jnp.concatenate([xp * low, xp * high], 0)
        yi_o[:, LANES * p : LANES * (p + 1)] = dot(jnp.concatenate(mixes, 1), blocks)


def finish_kernel(
    yi, xs, bc, cum, match, sin_l, pref, dev, z_ref, gains, expand, y_o, no_o, sin_o
):
    sin = (sin_l[0].astype(f32) + pref[0, 0:1, :] * dev[...]).astype(bf16)
    sin_o[0] = sin
    carry = widen(jnp.exp(cum[...]) * match[:, 4:5], expand[...])
    y = yi[...] + carry * dot(bc[:, N:], sin) + gains[1:2, :] * xs[...].astype(f32)
    y_o[...] = y
    z = z_ref[...]
    g = y * z * sigmoid(z)
    r = lax.rsqrt(jnp.mean(g * g, -1, keepdims=True) + EPS)
    no_o[...] = (g * r * gains[0:1, :]).astype(bf16)


def gate_back_kernel(
    gno, y_ref, z_ref, gains, cum, match, bc, pref, expand, dy_o, dz_o, edy_o, og_o, ds_o
):
    @pl.when(pl.program_id(0) == 0)
    def _():
        og_o[...] = jnp.zeros_like(og_o)
        ds_o[...] = jnp.zeros_like(ds_o)

    z = z_ref[...]
    y = y_ref[...]
    sz = sigmoid(z)
    silu = z * sz
    g = y * silu
    r = lax.rsqrt(jnp.mean(g * g, -1, keepdims=True) + EPS)
    gr = g * r
    gv = gno[...]
    og_o[...] += jnp.broadcast_to(jnp.sum(gv * gr, 0, keepdims=True), og_o.shape)
    gn = gv * gains[0:1, :]
    dg = r * (gn - gr * jnp.mean(gn * gr, -1, keepdims=True))
    dy = dg * silu
    dy_o[...] = dy.astype(bf16)
    dz_o[...] = (dg * y * sz * (1.0 + z * (1.0 - sz))).astype(bf16)
    edy = (widen(jnp.exp(cum[...]) * match[:, 4:5], expand[...]) * dy).astype(bf16)
    edy_o[...] = edy
    ds_o[...] += pref[0, 0:1, :] * dot(bc[:, N:], edy, COLS)


def intra_back_kernel(
    dy, xt, bc, cum, cumt, match, segt, reduce, dxi_o, dbc_o, dcum_o, rs
):
    rows = xt.shape[0]
    mask = decay_mask(match[:, 3:4], segt[0], True)
    b = bc[:, :N]
    c = bc[:, N:]
    scores = dot(b, c, ROWS)
    low, high = half_masks(rows)
    rs[...] = jnp.zeros_like(rs)
    dscores = jnp.zeros((rows, rows), f32)
    for p in range(xt.shape[1] // LANES):
        xp = xt[:, LANES * p : LANES * (p + 1)]
        dyp = dy[:, LANES * p : LANES * (p + 1)]
        dmix = dot(jnp.concatenate([xp * low, xp * high], 0), dyp, ROWS)
        mixes = []
        for j in range(2):
            h = 2 * p + j
            gap = cumt[0, h : h + 1, :] - cum[:, h : h + 1]
            decay = jnp.exp(jnp.where(mask, gap, MASKED))
            dm = dmix[rows * j : rows * (j + 1)]
            dscores = dscores + dm * decay
            mix = (decay * scores).astype(bf16)
            mixes.append(mix)
            rs[h : h + 1, :] = jnp.sum(dm * mix.astype(f32), 0, keepdims=True)
        blocks = jnp.concatenate([dyp * low, dyp * high], 0)
        dxi_o[:, LANES * p : LANES * (p + 1)] = dot(jnp.concatenate(mixes, 1), blocks)
    ds = dscores.astype(bf16)
    dbc_o[:, :N] = dot(ds, c)
    dbc_o[:, N:] = dot(ds, b, COLS)
    heads = cum.shape[1]
    cols = narrow_exact(xt[...].astype(f32) * dxi_o[...], reduce[...])
    dcum_o[...] = jnp.transpose(rs[...])[:, :heads] - cols


def sweep_kernel(
    dxi, dbc, dcum, dy, edy, dz, xt, bc, cum, match, sin_ref, proj, before, rim, convp, headp,
    gains, expand, reduce, dsn, gp_o, convg_o, headg_o, rim_o, ds, pad, buf, carry, acc,
):
    i = pl.program_id(0)
    steps = pl.num_programs(0)
    rows = xt.shape[0]
    heads = cum.shape[1]

    @pl.when(i == 0)
    def _():
        ds[...] = dsn[...]
        carry[...] = jnp.zeros_like(carry)
        convg_o[...] = jnp.zeros_like(convg_o)
        headg_o[...] = jnp.zeros_like(headg_o)

    @pl.when(i == steps - 1)
    def _():
        pad[0:8, :] = rim[...]

    @pl.when(i < steps - 1)
    def _():
        pad[0:8, :] = before[:, DI : DI + XC]

    pad[8 : 8 + rows, :] = proj[:, DI : DI + XC]
    m = match[...]
    conv = conv_forward(pad, m, convp, rows)
    sc = sigmoid(conv)
    act = conv * sc
    x = act[:, :DI]
    raw = proj[:, DI + XC : DI + XC + heads] + headp[0:1, :]
    dt = softplus(raw)
    rate = headp[1:2, :]
    cumv = cum[...]
    last = cumv[rows - 1 : rows, :]
    thru = jnp.exp(last) * m[rows - 1 : rows, 4:5]
    wide = widen(
        jnp.concatenate(
            [dt, jnp.exp(last - cumv) * m[:, 5:6], jnp.broadcast_to(thru, (8, heads))], 0
        ),
        expand[...],
    )
    dt_e = wide[:rows]
    tail_e = wide[rows : 2 * rows]
    thru_e = wide[2 * rows : 2 * rows + 1]
    b = bc[:, :N]
    c = bc[:, N:]
    state_grad = ds[...]
    low_grad = state_grad.astype(bf16)
    sin = sin_ref[0]
    xtv = xt[...].astype(f32)
    dyv = dy[...].astype(f32)
    edyb = edy[...]
    dx_in = tail_e * dot(b, low_grad)
    dxt = dxi[...] + dx_in
    stacked = jnp.concatenate(
        [
            (xtv * dx_in).astype(bf16),
            (edyb.astype(f32) * dot(c, sin)).astype(bf16),
            (x * dxt).astype(bf16),
            (x * dyv).astype(bf16),
        ],
        0,
    )
    sums = dot(stacked, reduce[...])
    db = dbc[:, :N] + dot((tail_e * xtv).astype(bf16), low_grad, ROWS)
    dc = dbc[:, N:] + dot(edyb, sin, ROWS)
    held = jnp.sum(state_grad * sin.astype(f32), 0, keepdims=True)
    dthru = narrow_exact(jnp.broadcast_to(held, (8, held.shape[1])), reduce[...])[0:1] * thru
    ds[...] = thru_e * state_grad + dot(c, edyb, COLS)
    row = lax.broadcasted_iota(jnp.int32, (rows, rows), 0)
    col = lax.broadcasted_iota(jnp.int32, (rows, rows), 1)
    dlog = (
        dot(jnp.where(row <= col, 1.0, 0.0), dcum[...] + sums[rows : 2 * rows], precision=highest)
        + dot(jnp.where(row > col, 1.0, 0.0), sums[:rows], precision=highest)
        + dthru
    )
    ddt = sums[2 * rows : 3 * rows] + dlog * rate
    draw = ddt * sigmoid(raw)
    headg_o[0:1, :] += jnp.sum(draw, 0, keepdims=True)
    headg_o[1:2, :] += jnp.sum(dlog * dt, 0, keepdims=True) * rate
    headg_o[2:3, :] += jnp.sum(sums[3 * rows :], 0, keepdims=True)
    gp_o[:, :DI] = dz[...]
    gp_o[:, DI + XC :] = jnp.zeros((rows, gp_o.shape[1] - DI - XC), bf16)
    gp_o[:, DI + XC : DI + XC + heads] = draw.astype(bf16)
    dact = jnp.concatenate([dt_e * dxt + gains[1:2, :] * dyv, db, dc], 1)
    dconv = dact * (sc * (1.0 + conv * (1.0 - sc)))
    convg_o[4:5, :] += jnp.sum(dconv, 0, keepdims=True)
    convg_o[3:4, :] += jnp.sum(dconv * pad[8 : 8 + rows, :], 0, keepdims=True)
    acc[...] = dconv * convp[3:4, :]
    rim_sum = jnp.zeros((8, XC), f32)
    for k in range(3):
        v = dconv * m[:, k : k + 1]
        convg_o[k : k + 1, :] += jnp.sum(v * pad[5 + k : 5 + k + rows, :], 0, keepdims=True)
        v = v * convp[k : k + 1, :]
        buf[0:8, :] = jnp.zeros((8, XC), f32)
        buf[8 : 8 + rows, :] = v
        buf[8 + rows : 16 + rows, :] = carry[8 * k : 8 * k + 8, :]
        shift = 3 - k
        acc[...] += buf[8 + shift : 8 + shift + rows, :]
        rim_sum = rim_sum + buf[shift : 8 + shift, :]
        carry[8 * k : 8 * k + 8, :] = v[0:8, :]
    gp_o[:, DI : DI + XC] = acc[...].astype(bf16)
    rim_o[...] = rim_sum


def shapes(*specs):
    return [jax.ShapeDtypeStruct(s, d) for s, d in specs]


def by_chunk(rows, cols, steps=None):
    if steps is None:
        return pl.BlockSpec((rows, cols), lambda i: (i, 0))
    return pl.BlockSpec((rows, cols), lambda i: (steps - 1 - i, 0))


def by_lead(a, b, steps=None):
    if steps is None:
        return pl.BlockSpec((1, a, b), lambda i: (i, 0, 0))
    return pl.BlockSpec((1, a, b), lambda i: (steps - 1 - i, 0, 0))


def fixed(*shape):
    return pl.BlockSpec(shape, lambda i: (0,) * len(shape))


def call(kernel, steps, ins, outs, out_shape, scratch=()):
    return pl.pallas_call(
        kernel,
        grid=(steps,),
        in_specs=ins,
        out_specs=outs,
        out_shape=out_shape,
        scratch_shapes=scratch,
        compiler_params=pltpu.CompilerParams(
            dimension_semantics=("arbitrary",), vmem_limit_bytes=VMEM_LIMIT
        ),
        cost_estimate=pl.CostEstimate(flops=1000, bytes_accessed=1000, transcendentals=0),
    )


def shifted(value, axis, steps):
    count = lax.axis_size(axis)
    initial, last = (max(0, -steps), min(count, count - steps))
    return lax.ppermute(value, axis, [(source, source + steps) for source in range(initial, last)])


def relay(through, local, steps):
    incoming = shifted(local, "seq", steps)
    for _ in range(lax.axis_size("seq") - 2):
        incoming = shifted(through[0:1] * incoming + local, "seq", steps)
    return incoming


def rms_scale(values, gain):
    return values * lax.rsqrt(jnp.mean(values * values, -1, keepdims=True) + EPS) * gain


def layer_forward(source, w, seg):
    match, segt, rows = seg["match"], seg["segt"], seg["rows"]
    T = source.shape[0]
    nc = T // rows
    H = w["headp"].shape[1]
    PWL = w["win"].shape[1]
    normed = rms_scale(source, w["norm_gain"]).astype(bf16)
    proj = dot(normed, w["win"])
    rim = shifted(proj[-8:, DI : DI + XC], "seq", 1)
    expand = seg["expand"]
    xt, xs, bc, cum, cumt, sin_l, end, pref, thru = call(
        prep_kernel,
        nc,
        [by_chunk(rows, PWL), fixed(8, XC), by_chunk(rows, 8), fixed(8, XC), fixed(8, H),
         fixed(*expand.shape)],
        [by_chunk(rows, DI), by_chunk(rows, DI), by_chunk(rows, 2 * N), by_chunk(rows, H),
         by_lead(H, rows), by_lead(N, DI), fixed(N, DI), by_lead(8, DI), fixed(8, DI)],
        shapes(((T, DI), bf16), ((T, DI), bf16), ((T, 2 * N), bf16), ((T, H), f32),
               ((nc, H, rows), f32), ((nc, N, DI), bf16), ((N, DI), f32), ((nc, 8, DI), f32),
               ((8, DI), f32)),
        [pltpu.VMEM((rows + 8, XC), f32), pltpu.VMEM((N, DI), f32), pltpu.VMEM((8, DI), f32)],
    )(proj, rim, match, w["convp"], w["headp"], expand)
    dev = relay(thru, end, 1)
    yi = call(
        intra_kernel,
        nc,
        [by_chunk(rows, DI), by_chunk(rows, 2 * N), by_chunk(rows, H), by_lead(H, rows),
         by_chunk(rows, 8), by_lead(1, rows)],
        by_chunk(rows, DI),
        jax.ShapeDtypeStruct((T, DI), f32),
    )(xt, bc, cum, cumt, match, segt)
    y, normed_out, sin = call(
        finish_kernel,
        nc,
        [by_chunk(rows, DI), by_chunk(rows, DI), by_chunk(rows, 2 * N), by_chunk(rows, H),
         by_chunk(rows, 8), by_lead(N, DI), by_lead(8, DI), fixed(N, DI), by_chunk(rows, DI),
         fixed(8, DI), fixed(*expand.shape)],
        [by_chunk(rows, DI), by_chunk(rows, DI), by_lead(N, DI)],
        shapes(((T, DI), f32), ((T, DI), bf16), ((nc, N, DI), bf16)),
    )(yi, xs, bc, cum, match, sin_l, pref, dev, proj, w["gains"], expand)
    out = source + dot(normed_out, w["wout"])
    kept = dict(
        source=source, normed=normed, proj=proj, rim=rim, xt=xt, bc=bc, cum=cum, cumt=cumt,
        pref=pref, thru=thru, y=y, normed_out=normed_out, sin=sin,
    )
    return out, kept


def layer_backward(grad_low, w, seg, kept, beside):
    match, segt, rows = seg["match"], seg["segt"], seg["rows"]
    T = grad_low.shape[0]
    nc = T // rows
    H = w["headp"].shape[1]
    PWL = w["win"].shape[1]
    expand, reduce = seg["expand"], seg["reduce"]
    proj, bc, cum, xt = kept["proj"], kept["bc"], kept["cum"], kept["xt"]
    grad_low = move(beside, grad_low)
    out_sums, grad_low = fold([kept["normed_out"]], lambda g: [g], grad_low, bool(beside))
    gno = dot(grad_low, w["wout"], ROWS)
    dy, dz, edy, og, ds_local = call(
        gate_back_kernel,
        nc,
        [by_chunk(rows, DI), by_chunk(rows, DI), by_chunk(rows, DI), fixed(8, DI),
         by_chunk(rows, H), by_chunk(rows, 8), by_chunk(rows, 2 * N), by_lead(8, DI),
         fixed(*expand.shape)],
        [by_chunk(rows, DI), by_chunk(rows, DI), by_chunk(rows, DI), fixed(8, DI), fixed(N, DI)],
        shapes(((T, DI), bf16), ((T, DI), bf16), ((T, DI), bf16), ((8, DI), f32), ((N, DI), f32)),
    )(gno, kept["y"], proj, w["gains"], cum, match, bc, kept["pref"], expand)
    dy = move([out_sums] + beside[1:], dy)
    dsn = relay(kept["thru"], ds_local, -1)
    dxi, dbc, dcum = call(
        intra_back_kernel,
        nc,
        [by_chunk(rows, DI), by_chunk(rows, DI), by_chunk(rows, 2 * N), by_chunk(rows, H),
         by_lead(H, rows), by_chunk(rows, 8), by_lead(1, rows), fixed(*reduce.shape)],
        [by_chunk(rows, DI), by_chunk(rows, 2 * N), by_chunk(rows, H)],
        shapes(((T, DI), f32), ((T, 2 * N), f32), ((T, H), f32)),
        [pltpu.VMEM((LANES, rows), f32)],
    )(dy, xt, bc, cum, kept["cumt"], match, segt, reduce)
    dxi = move(beside, dxi)
    rc = partial(by_chunk, rows, steps=nc)
    gp, convg, headg, rim_grad = call(
        sweep_kernel,
        nc,
        [rc(DI), rc(2 * N), rc(H), rc(DI), rc(DI), rc(DI), rc(DI), rc(2 * N), rc(H), rc(8),
         by_lead(N, DI, nc), rc(PWL),
         pl.BlockSpec((8, PWL), lambda i: (jnp.maximum((nc - 1 - i) * (rows // 8) - 1, 0), 0)),
         fixed(8, XC), fixed(8, XC), fixed(8, H), fixed(8, DI), fixed(*expand.shape),
         fixed(*reduce.shape), fixed(N, DI)],
        [rc(PWL), fixed(8, XC), fixed(8, H), fixed(8, XC)],
        shapes(((T, PWL), bf16), ((8, XC), f32), ((8, H), f32), ((8, XC), f32)),
        [pltpu.VMEM((N, DI), f32), pltpu.VMEM((rows + 8, XC), f32),
         pltpu.VMEM((rows + 16, XC), f32), pltpu.VMEM((24, XC), f32),
         pltpu.VMEM((rows, XC), f32)],
    )(dxi, dbc, dcum, dy, edy, dz, xt, bc, cum, match, kept["sin"], proj, proj, kept["rim"],
      w["convp"], w["headp"], w["gains"], expand, reduce, dsn)
    gp = move([out_sums] + beside, gp)
    returned = shifted(rim_grad, "seq", -1)
    tail = (gp[-16:, DI : DI + XC].astype(f32)
            + jnp.concatenate([jnp.zeros_like(returned), returned], 0)).astype(bf16)
    gp = lax.dynamic_update_slice(gp, tail, (T - 16, DI))
    half = PWL // 2
    in_sums, gp = fold([kept["normed"]] * 2, lambda g: [g[:, :half], g[:, half:]], gp, bool(beside))
    if beside:
        gp = move([in_sums, out_sums] + beside, gp)
    grad_normed = dot(gp, w["win"], ROWS)
    if beside:
        grad_normed = move([in_sums], grad_normed)
    _, norm_pull = jax.vjp(rms_scale, kept["source"], w["norm_gain"])
    grad_source, grad_norm_gain = norm_pull(grad_normed)
    return grad_source, [in_sums, out_sums], (grad_norm_gain, convg, og[0], headg)


def bit_of(axis, bit):
    return (lax.axis_index(axis) // bit) % 2 == 1


def swap(value, axis, bit):
    return lax.ppermute(value, axis, [(i, i ^ bit) for i in range(lax.axis_size(axis))])


def bits(axis):
    count = lax.axis_size(axis)
    return [(axis, 1 << k) for k in reversed(range(count.bit_length() - 1))]


class Chains:
    def __init__(self, keeps, received, last):
        x = [("section", 1)]
        dp_bits = bits("dp")
        low, mid, rest = dp_bits[-1:], dp_bits[-2:-1], dp_bits[:-2]
        more = rest + bits("seq")[1:]
        if len(keeps) == 1:
            self.orders = [low + x + mid + more]
        elif last:
            self.orders = [mid + low + x + more, low + mid + x + more]
        else:
            self.orders = [mid + x + low + more, low + mid + x + more]
        self.dims = [bits("seq")[1:] + dp_bits for _ in keeps]
        self.flying = list(zip(keeps, received))

    def parts(self):
        keeps, sends, steps = [], [], []
        for k, value in enumerate(self.values):
            step = self.orders[k].pop(0)
            mine = bit_of(*step)
            if step[0] == "section":
                half = value.shape[-1] // 2
                one, two = value[..., :half], value[..., half:]
                keep, send = jnp.where(mine, two, one), jnp.where(mine, one, two)
            else:
                dims = self.dims[k]
                d = dims.index(step)
                dims.remove(step)
                rows = value.shape[-2] >> (len(dims) + 1)
                grid = value.reshape((2,) * (len(dims) + 1) + (rows, value.shape[-1]))
                own = mine.astype(jnp.int32)
                keep = lax.dynamic_index_in_dim(grid, own, d, keepdims=False)
                send = lax.dynamic_index_in_dim(grid, 1 - own, d, keepdims=False)
                keep, send = (v.reshape(-1, v.shape[-1]) for v in (keep, send))
            keeps.append(keep)
            sends.append(send.astype(bf16))
            steps.append(step)
        return keeps, sends, steps

    def left(self):
        return bool(self.orders[0])


class Whole:
    def __init__(self, value):
        self.flying = []
        self.values = [value]
        self.order = bits("seq") + bits("dp")[::-1] + bits("section")

    def parts(self):
        return self.values, self.values, [self.order.pop(0)]

    def left(self):
        return bool(self.order)


def spread(values):
    section, seq, dp = bits("section"), bits("seq"), bits("dp")
    present = []
    for step in dp[:-2] + dp[-2:-1] + section + dp[-1:] + seq:
        place = sum((section + seq + dp).index(p) < (section + seq + dp).index(step) for p in present)
        present.append(step)
        mine = bit_of(*step)
        got = [swap(v, *step) for v in values]
        values = [
            jnp.stack([jnp.where(mine, g, v), jnp.where(mine, v, g)], place)
            for v, g in zip(values, got)
        ]
    return values


def fold(lefts, rights, anchor, last):
    top = bits("seq")[0]
    mine = bit_of(*top)
    halves = [(v[:, : v.shape[1] // 2], v[:, v.shape[1] // 2 :]) for v in lefts]
    sends = [
        dot(jnp.where(mine, low, high), r, COLS).astype(bf16)
        for (low, high), r in zip(halves, rights(anchor))
    ]
    anchor, sends = lax.optimization_barrier((anchor, sends))
    received = [swap(v, *top) for v in sends]
    keeps = [
        dot(jnp.where(mine, high, low), r, COLS) for (low, high), r in zip(halves, rights(anchor))
    ]
    return Chains(keeps, received, last), anchor


def launch(chains, anchor):
    parts = [c.parts() for c in chains]
    anchor, sends = lax.optimization_barrier((anchor, [p[1] for p in parts]))
    for c, (keeps, _, steps), out in zip(chains, parts, sends):
        c.flying = [(k, swap(s, *step)) for k, s, step in zip(keeps, out, steps)]
    return anchor


def land(chains, anchor):
    received = [[r for _, r in c.flying] for c in chains]
    anchor, received = lax.optimization_barrier((anchor, received))
    for c, got in zip(chains, received):
        c.values = [k + r.astype(f32) for (k, _), r in zip(c.flying, got)]
        c.flying = []
    return anchor


def move(chains, anchor):
    chains = [c for c in chains if c.flying]
    if not chains:
        return anchor
    anchor = land(chains, anchor)
    chains = [c for c in chains if c.left()]
    return launch(chains, anchor) if chains else anchor


def seg_tables(segments, rows, heads):
    T = segments.shape[0]
    seg = segments.astype(f32)
    rim = shifted(seg[-3:], "seq", 1)
    padded = jnp.concatenate([rim, seg])
    cols = [(padded[k : k + T] == seg).astype(f32) for k in range(3)]
    chunked = seg.reshape(-1, rows)
    ends = chunked[:, -1]
    starts = jnp.concatenate([rim[-1:], ends[:-1]])
    cols.append(seg)
    cols.append((chunked == starts[:, None]).astype(f32).reshape(-1))
    cols.append((chunked == ends[:, None]).astype(f32).reshape(-1))
    match = jnp.stack(cols + [jnp.zeros_like(seg)] * 2, 1)
    head_of = jnp.arange(DI) // (DI // heads)
    one = (jnp.arange(heads)[:, None] == head_of[None, :]).astype(bf16)
    return dict(
        match=match, segt=chunked[:, None, :], rows=rows,
        expand=jnp.concatenate([one, one, one], 0), reduce=one.T,
    )


def shards(
    tokens, cotangent, segments, norm_gain, in_weight, conv_weight, conv_bias, dt_bias, decay_log,
    skip_gain, out_gain, out_weight,
):
    section = lax.axis_index("section")
    is_first = section == 0
    D = tokens.shape[-1]
    H = dt_bias.shape[-1]
    T = tokens.shape[2]
    rows = min(LANES, T)
    cut = conv_weight.shape[-1]
    everyone = ("section", "seq", "dp")
    mine = partial(lax.dynamic_index_in_dim, index=section, axis=0, keepdims=False)
    source = mine(tokens)[0]
    grad_low = mine(cotangent)[0]
    seg = seg_tables(mine(segments)[0], rows, H)

    small = jnp.concatenate(
        [norm_gain[0], conv_weight[0].reshape(-1), conv_bias[0], out_gain[0]]
    )[None]
    wout, small = spread([out_weight[0], small])
    wout = wout.reshape(2, DI, D)
    small = small.reshape(2, -1, small.shape[-1]).astype(f32)
    heads_own = jnp.concatenate([dt_bias, -jnp.exp(decay_log), skip_gain], 0)
    heads_other = lax.ppermute(heads_own, "section", [(0, 1), (1, 0)])
    width = -(-in_weight.shape[2] // (4 * LANES)) * 4 * LANES
    padded = jnp.pad(in_weight, ((0, 0), (0, 0), (0, width - in_weight.shape[2])))
    win = lax.all_gather(padded, everyone, axis=1, tiled=True).reshape(2, D, -1)
    weights = []
    nd, no = norm_gain.shape[-1], out_gain.shape[-1]
    for s in range(2):
        vec = small[s]
        heads = jnp.where(section == s, heads_own, heads_other)
        taps = vec[:, nd : nd + 4 * cut].reshape(-1, 4, cut)
        taps = jnp.swapaxes(taps, 0, 1).reshape(4, -1)
        bias = vec[:, nd + 4 * cut : nd + 5 * cut].reshape(1, -1)
        gain = vec[:, nd + 5 * cut :].reshape(1, -1)
        skip = jnp.repeat(heads[2], DI // H)[None]
        weights.append(dict(
            norm_gain=vec[:, :nd].reshape(-1),
            convp=jnp.concatenate([taps, bias, jnp.zeros((3, XC), f32)], 0),
            headp=jnp.concatenate([heads, jnp.zeros((5, H), f32)], 0),
            gains=jnp.concatenate([gain, skip, jnp.zeros((6, DI), f32)], 0),
            win=win[s], wout=wout[s],
        ))

    out0, kept0 = layer_forward(source.astype(f32), weights[0], seg)
    passed = out0.astype(bf16)
    out1, kept1 = layer_forward(passed.astype(f32), weights[1], seg)
    final = out1.astype(bf16)
    got_out = swap(jnp.where(is_first, final, passed), "section", 1)

    grad1, beside, terms1 = layer_backward(grad_low, weights[1], seg, kept1, [])
    middle = (grad_low.astype(f32) + grad1).astype(bf16)
    middle, got_out = lax.optimization_barrier((middle, got_out))
    got_middle = lax.ppermute(middle, "section", [(0, 1)])
    grad0, sums, terms0 = layer_backward(middle, weights[0], seg, kept0, beside)
    first = middle.astype(f32) + grad0
    got_first = lax.ppermute(first.astype(bf16), "section", [(1, 0)])

    def both(position):
        return jnp.stack([terms0[position], terms1[position]])

    convg = both(1)
    packed = jnp.concatenate(
        [both(0).reshape(2, -1, nd),
         jnp.swapaxes(convg[:, :4].reshape(2, 4, -1, cut), 1, 2).reshape(2, -1, 4 * cut),
         convg[:, 4].reshape(2, -1, cut), both(2).reshape(2, -1, no)], -1
    )
    spare = packed.shape[-1] - 3 * H
    head_sums = jnp.pad(both(3)[:, :3].reshape(2, 1, -1), ((0, 0), (0, 0), (0, spare)))
    small = Whole(jnp.concatenate([packed, head_sums], 1))

    def join(zero, one):
        own, other = jnp.where(is_first, zero, one), jnp.where(is_first, one, zero)
        other = swap(other.astype(bf16), "section", 1).astype(f32)
        return [jnp.where(is_first, own, other), jnp.where(is_first, other, own)]

    for _ in range(2):
        launch([small], ())
        land([small], ())
    in1, out1 = beside
    in0, out0 = sums
    grad_out = None
    running = [in0, out0, in1, out1, small]
    while running:
        got_first = move(running, got_first)
        running = [c for c in running if c.flying or c.left()]
        waiting = [c for c in running if not c.flying]
        if waiting:
            launch(waiting, ())
        if grad_out is None and out0 not in running and out1 not in running:
            grad_out = join(out0.values[0], out1.values[0])
    section_outputs = jnp.stack(
        [jnp.where(is_first, passed, got_out), jnp.where(is_first, got_out, final)]
    )
    input_grads = jnp.stack(
        [jnp.where(is_first, first, got_middle.astype(f32)),
         jnp.where(is_first, got_first, middle).astype(f32)]
    )
    packed = jnp.where(is_first, small.values[0][0], small.values[0][1])
    head_sums = packed[-1, : 3 * H].reshape(3, H)
    place = lax.axis_index("seq") * lax.axis_size("dp") + lax.axis_index("dp")
    vec = lax.dynamic_index_in_dim(packed, place, 0, keepdims=False)
    grad_in = join(in0.values[0], in1.values[0]) + join(in0.values[1], in1.values[1])
    grad_in = jnp.concatenate(grad_in, -1)[None, :, : in_weight.shape[2]]
    grad_out = jnp.concatenate(grad_out, -1)[None]
    return (
        section_outputs[None, :, None],
        input_grads[None, :, None],
        vec[None, :nd],
        grad_in,
        vec[nd : nd + 4 * cut].reshape(1, 4, cut),
        vec[None, nd + 4 * cut : nd + 5 * cut],
        head_sums[0:1],
        head_sums[1:2],
        head_sums[2:3],
        vec[None, nd + 5 * cut :],
        grad_out,
    )


def solution(mesh):
    placed = (
        P(None, "dp", "seq", None),
        P(None, "dp", "seq", None),
        P(None, "dp", "seq"),
        P("section", ("seq", "dp")),
        P("section", ("seq", "dp"), None),
        P("section", None, ("seq", "dp")),
        P("section", ("seq", "dp")),
        P("section", None),
        P("section", None),
        P("section", None),
        P("section", ("seq", "dp")),
        P("section", ("seq", "dp"), None),
    )
    return jax.shard_map(
        shards,
        mesh=mesh,
        in_specs=placed,
        out_specs=(
            P("section", None, "dp", "seq", None),
            P("section", None, "dp", "seq", None),
            P("section", ("seq", "dp")),
            P("section", ("seq", "dp"), None),
            P("section", None, ("seq", "dp")),
            P("section", ("seq", "dp")),
            P("section", None),
            P("section", None),
            P("section", None),
            P("section", ("seq", "dp")),
            P("section", ("seq", "dp"), None),
        ),
        check_vma=False,
    )
```
